32 devices in a mesh: groups: 2 (over y), rows: 4 (over x, core), cols: 4 (over z).
Axes of the slice: x: 2, y: 2, z: 4, core: 2. Of those that a mesh axis runs over, the one named last changes fastest.
Arguments:
- contact_map: bfloat16 [128, 64, 128], P(('groups', 'rows'), 'cols'), parts along dimension 0, may hold values from -6 to 6
- w_near: bfloat16 [2, 3, 3, 128, 128], replicated, may hold values from -0.1875 to 0.1875
- w_far: bfloat16 [2, 3, 3, 128, 128], replicated, may hold values from -0.1875 to 0.1875
Outputs:
- refined_map: bfloat16 [128, 64, 128], P(('groups', 'rows'), 'cols'), parts along dimension 0
The draws below stay inside these ranges and needn't reach their ends.
There are 2 independent parts, one for each index of `groups`. The reference program is written for one: setup_inputs(seed, part) draws one part's arguments, and reference() takes and returns one part's arrays. A program takes and returns all parts, laid end to end along the dimension named above; an argument that names none is the same for every part. Nothing has to cross between parts.
All inputs are finite; a program needn't handle non-finite values.
Results may differ from the reference program's by a relative error of at most 0.0066.
Values may be sent and summed in bfloat16 or wider, within the bound.
A program may use at most 64 MiB of HBM per device.

```python
import jax
import jax.numpy as jnp
from jax import lax

C = 128
BLOCKS = 2
L = 64


def shard_levels(own_key, shape, shards, least, high):
    level, own = 1.0, jax.random.fold_in(own_key, 6)
    for axis_at, blocks in shards:
        draws = jnp.exp(jax.random.uniform(jax.random.fold_in(own, axis_at), (blocks,), jnp.float32, least / len(shards), high / len(shards)))
        level = level * jnp.repeat(draws, shape[axis_at] // blocks).reshape([-1 if axis == axis_at else 1 for axis in range(len(shape))])
    return level


def centred(rng, extent, width, limit, shards=(), kind=jnp.bfloat16):
    result = width * jax.random.normal(rng, extent, jnp.float32)
    if shards:
        result = result * shard_levels(rng, extent, shards, -0.22, 0.18)
    return jnp.clip(result, -limit, limit).astype(kind)


def setup_inputs(seed: int = 0, part: int = 0) -> dict:
    splits = jax.random.split(jax.random.key(seed), 4)
    part_splits = jax.random.split(jax.random.fold_in(splits[3], part), 4)
    return {
        "contact_map": centred(part_splits[0], (L, L, C), 1.0, 6.0, ((0, 4), (1, 4))),
        "w_near": centred(splits[1], (BLOCKS, 3, 3, C, C), (9 * C) ** -0.5, 0.1875),
        "w_far": centred(splits[2], (BLOCKS, 3, 3, C, C), (9 * C) ** -0.5, 0.1875),
    }


def dilated(values, kernel, spread):
    out = lax.conv_general_dilated(values[None].astype(jnp.float32), kernel.astype(jnp.float32), (1, 1), [(spread, spread), (spread, spread)], rhs_dilation=(spread, spread), dimension_numbers=("NHWC", "HWIO", "NHWC"), preferred_element_type=jnp.float32)
    return out[0]


def reference(contact_map, w_near, w_far):
    state = contact_map
    for block in range(BLOCKS):
        hidden = jax.nn.relu(dilated(state, w_near[block], 2)).astype(jnp.bfloat16)
        block_out = (state.astype(jnp.float32) + dilated(hidden, w_far[block], 4)).astype(jnp.bfloat16)
        mirrored = jnp.swapaxes(block_out, 0, 1)
        state = ((block_out.astype(jnp.float32) + mirrored.astype(jnp.float32)) * 0.5).astype(jnp.bfloat16)
    return state
```

```python
import functools

import jax
import jax.numpy as jnp
from jax import lax
from jax.experimental import pallas as pl
from jax.experimental.pallas import tpu as pltpu
from jax.sharding import PartitionSpec as P

MESH = pl.DeviceIdType.MESH
NEAR, FAR = 2, 4
HALO = NEAR + FAR
PAD = 16
SIDES = [(-1, 0), (1, 0), (0, -1), (0, 1), (-1, -1), (-1, 1), (1, -1), (1, 1)]


def extended(cells, sides, width):
    for axis, dim in sides:
        count = lax.axis_size(axis)
        ends = count - 1
        head = lax.slice_in_dim(cells, 0, width, axis=dim)
        tail = lax.slice_in_dim(cells, cells.shape[dim] - width, cells.shape[dim], axis=dim)
        cells = jnp.concatenate(
            [
                lax.ppermute(tail, axis, [(i, (i + 1) % count) for i in range(ends)]),
                cells,
                lax.ppermute(head, axis, [((i + 1) % count, i) for i in range(ends)]),
            ],
            axis=dim,
        )
    return cells


def valid_conv(padded, kernel, spread):
    out = lax.conv_general_dilated(
        padded[None],
        kernel,
        (1, 1),
        "VALID",
        rhs_dilation=(spread, spread),
        dimension_numbers=("NHWC", "HWIO", "NHWC"),
        preferred_element_type=jnp.float32,
    )
    return out[0]


def average(block_out, flipped):
    return ((block_out.astype(jnp.float32) + flipped.astype(jnp.float32)) * 0.5).astype(
        jnp.bfloat16
    )


def by_rows(contact_map, w_near, w_far):
    blocks = w_near.shape[0]
    state = lax.all_to_all(contact_map, "cols", split_axis=0, concat_axis=1, tiled=True)
    for block in range(blocks):
        padded = extended(state, ((("rows", "cols"), 0),), NEAR)
        padded = jnp.pad(padded, ((0, 0), (NEAR, NEAR), (0, 0)))
        hidden = jax.nn.relu(valid_conv(padded, w_near[block], NEAR)).astype(jnp.bfloat16)
        padded = extended(hidden, ((("rows", "cols"), 0),), FAR)
        padded = jnp.pad(padded, ((0, 0), (FAR, FAR), (0, 0)))
        block_out = (state.astype(jnp.float32) + valid_conv(padded, w_far[block], FAR)).astype(
            jnp.bfloat16
        )
        mirrored = lax.all_to_all(
            block_out, ("rows", "cols"), split_axis=1, concat_axis=0, tiled=True
        )
        state = average(block_out, jnp.swapaxes(mirrored, 0, 1))
    return lax.all_to_all(state, "cols", split_axis=1, concat_axis=0, tiled=True)


def flip(cells):
    return jnp.transpose(cells, (1, 0, 2))


def tile_kernel(
    count, side, x_ref, near_ref, far_ref, out_ref,
    pads, turned, strips, mirror, near, far, load_sem, send_sem, recv_sem, mirror_sem,
):
    blocks, channels = near_ref.shape[0], near_ref.shape[-1]
    row, col = lax.axis_index("rows"), lax.axis_index("cols")
    last = count - 1
    inner = slice(HALO, HALO + side)
    body = slice(PAD, PAD + side)

    load = pltpu.make_async_copy(x_ref, pads.at[0, inner, body], load_sem.at[0])
    load.start()
    load_near = pltpu.make_async_copy(near_ref, near, load_sem.at[1])
    load_far = pltpu.make_async_copy(far_ref, far, load_sem.at[2])
    load_near.start()
    load_far.start()

    def there(step):
        di, dj = step
        ok = []
        if di:
            ok.append(row > 0 if di < 0 else row < last)
        if dj:
            ok.append(col > 0 if dj < 0 else col < last)
        return ok[0] if len(ok) == 1 else jnp.logical_and(*ok)

    barrier = pltpu.get_barrier_semaphore()
    friends = jnp.int32(0)
    for step in SIDES:
        yes = there(step)
        friends += yes.astype(jnp.int32)

        @pl.when(yes)
        def _():
            pl.semaphore_signal(
                barrier, inc=1, device_id={"rows": row + step[0], "cols": col + step[1]},
                device_id_type=MESH,
            )

    @pl.when(row != col)
    def _():
        pl.semaphore_signal(
            barrier, inc=1, device_id={"rows": col, "cols": row}, device_id_type=MESH
        )

    friends += (row != col).astype(jnp.int32)

    zero = functools.partial(jnp.zeros, dtype=jnp.bfloat16)
    wide = pads.shape[2]
    for n in range(blocks):
        @pl.when(row == 0)
        def _():
            pads[n, :HALO] = zero((HALO, wide, channels))

        @pl.when(row == last)
        def _():
            pads[n, HALO + side:] = zero((HALO, wide, channels))

        @pl.when(col == 0)
        def _():
            pads[n, :, :PAD] = zero((side + 2 * HALO, PAD, channels))

        @pl.when(col == last)
        def _():
            pads[n, :, PAD + side:] = zero((side + 2 * HALO, PAD, channels))

    load.wait()
    pl.semaphore_wait(barrier, friends)

    def rim_copy(n, at):
        di, dj = SIDES[at]
        if di:
            rows = slice(HALO, 2 * HALO) if di < 0 else slice(side, side + HALO)
            to = slice(HALO + side, 2 * HALO + side) if di < 0 else slice(0, HALO)
            start = PAD - dj * side
            source = pads.at[n, rows, body]
            target = pads.at[n, to, start:start + side]
        else:
            source = turned.at[n, 0 if dj < 0 else 1]
            target = strips.at[n, 1 if dj < 0 else 0]
        return pltpu.make_async_remote_copy(
            src_ref=source, dst_ref=target,
            send_sem=send_sem.at[n, at], recv_sem=recv_sem.at[n, at],
            device_id={"rows": row + di, "cols": col + dj}, device_id_type=MESH,
        )

    def rim(n):
        flat = flip(pads[n, inner, body])
        turned[n, 0] = flat[:HALO]
        turned[n, 1] = flat[side - HALO:]
        for at, step in enumerate(SIDES):
            @pl.when(there(step))
            def _():
                rim_copy(n, at).start()

    def rim_wait(n):
        for at, (di, dj) in enumerate(SIDES):
            @pl.when(there((-di, -dj)))
            def _():
                rim_copy(n, at).wait_recv()

        @pl.when(col > 0)
        def _():
            pads[n, inner, PAD - HALO:PAD] = flip(strips[n, 0])

        @pl.when(col < last)
        def _():
            pads[n, inner, PAD + side:PAD + side + HALO] = flip(strips[n, 1])

    reach = side + 2 * FAR
    span = side + PAD

    def hidden_of(n, weights):
        first = PAD - HALO
        taps = [
            pads[n, NEAR * a:NEAR * a + reach, first + NEAR * b:first + NEAR * b + span]
            .reshape(reach * span, channels)
            for a in range(3) for b in range(3)
        ]
        total = jnp.dot(
            jnp.concatenate(taps, axis=1), weights, preferred_element_type=jnp.float32
        )
        total = jnp.maximum(total, 0.0).reshape(reach, span, total.shape[-1])
        i = lax.broadcasted_iota(jnp.int32, total.shape, 0) + (row * side - FAR)
        j = lax.broadcasted_iota(jnp.int32, total.shape, 1) + (col * side - FAR)
        whole = count * side
        on_map = (i >= 0) & (i < whole) & (j >= 0) & (j < whole)
        return jnp.where(on_map, total, 0.0).astype(jnp.bfloat16)

    def block_out_of(n, hidden, weights):
        taps = [
            hidden[FAR * a:FAR * a + side, FAR * b:FAR * b + side]
            .reshape(side * side, channels)
            for a in range(3) for b in range(3)
        ]
        total = jnp.dot(
            jnp.concatenate(taps, axis=1), weights, preferred_element_type=jnp.float32
        ).reshape(side, side, channels)
        return (pads[n, inner, body].astype(jnp.float32) + total).astype(jnp.bfloat16)

    def straight(w, n):
        return w[n].reshape(9 * channels, channels)

    def crossed(w, n):
        return jnp.concatenate([w[n, b, a] for a in range(3) for b in range(3)], axis=0)

    rim(0)
    load_near.wait()
    load_far.wait()
    for n in range(blocks - 1):
        rim_wait(n)
        hidden = hidden_of(n, straight(near, n))
        block_out = block_out_of(n, hidden, straight(far, n))
        mirror[n, 0] = flip(block_out)
        swap = pltpu.make_async_remote_copy(
            src_ref=mirror.at[n, 0], dst_ref=mirror.at[n, 1],
            send_sem=mirror_sem.at[n, 0], recv_sem=mirror_sem.at[n, 1],
            device_id={"rows": col, "cols": row}, device_id_type=MESH,
        )

        @pl.when(row != col)
        def _():
            swap.start()
            swap.wait()

        @pl.when(row == col)
        def _():
            mirror[n, 1] = mirror[n, 0]

        pads[n + 1, inner, body] = average(block_out, mirror[n, 1])
        rim(n + 1)

    n = blocks - 1
    both = jnp.concatenate([straight(near, n), crossed(near, n)], axis=1)
    rim_wait(n)
    hidden = hidden_of(n, both)
    block_out = block_out_of(n, hidden[..., :channels], straight(far, n))
    flipped = block_out_of(n, hidden[..., channels:], crossed(far, n))
    out_ref[...] = average(block_out, flipped)

    for n in range(blocks):
        for at, step in enumerate(SIDES):
            @pl.when(there(step))
            def _():
                rim_copy(n, at).wait_send()


def by_tiles(contact_map, w_near, w_far):
    blocks, channels = w_near.shape[0], w_near.shape[-1]
    side, count = contact_map.shape[0], lax.axis_size("rows")
    kind = contact_map.dtype
    anywhere = pl.BlockSpec(memory_space=pl.ANY)
    return pl.pallas_call(
        functools.partial(tile_kernel, count, side),
        out_shape=jax.ShapeDtypeStruct(contact_map.shape, kind),
        in_specs=[anywhere] * 3,
        out_specs=pl.BlockSpec(memory_space=pltpu.VMEM),
        scratch_shapes=[
            pltpu.VMEM((blocks, side + 2 * HALO, side + 2 * PAD, channels), kind),
            pltpu.VMEM((blocks, 2, HALO, side, channels), kind),
            pltpu.VMEM((blocks, 2, HALO, side, channels), kind),
            pltpu.VMEM((blocks, 2, side, side, channels), kind),
            pltpu.VMEM(w_near.shape, kind),
            pltpu.VMEM(w_far.shape, kind),
            pltpu.SemaphoreType.DMA((3,)),
            pltpu.SemaphoreType.DMA((blocks, len(SIDES))),
            pltpu.SemaphoreType.DMA((blocks, len(SIDES))),
            pltpu.SemaphoreType.DMA((blocks, 2)),
        ],
        compiler_params=pltpu.CompilerParams(
            collective_id=0, has_side_effects=True, vmem_limit_bytes=32 * 2**20
        ),
    )(contact_map, w_near, w_far)


def on_device(contact_map, w_near, w_far):
    side = contact_map.shape[0]
    square = side == contact_map.shape[1] and side % PAD == 0
    if square and lax.axis_size("rows") == lax.axis_size("cols") and w_near.shape[0] > 1:
        return by_tiles(contact_map, w_near, w_far)
    return by_rows(contact_map, w_near, w_far)


def solution(mesh):
    in_specs = (P(("groups", "rows"), "cols", None), P(), P())
    out_specs = P(("groups", "rows"), "cols", None)
    return jax.shard_map(
        on_device, mesh=mesh, in_specs=in_specs, out_specs=out_specs, check_vma=False
    )
```

```python
import functools

import jax
import jax.numpy as jnp
from jax import lax
from jax.experimental import pallas as pl
from jax.experimental.pallas import tpu as pltpu
from jax.sharding import PartitionSpec as P

MESH = pl.DeviceIdType.MESH
NEAR, FAR = 2, 4
HALO = NEAR + FAR
PAD, PACK = 16, 8
SIDES = [(0, -1), (0, 1), (-1, -1), (-1, 1), (1, -1), (1, 1), (-1, 0), (1, 0)]


def extended(cells, sides, width):
    for axis, dim in sides:
        count = lax.axis_size(axis)
        ends = count - 1
        head = lax.slice_in_dim(cells, 0, width, axis=dim)
        tail = lax.slice_in_dim(cells, cells.shape[dim] - width, cells.shape[dim], axis=dim)
        cells = jnp.concatenate(
            [
                lax.ppermute(tail, axis, [(i, (i + 1) % count) for i in range(ends)]),
                cells,
                lax.ppermute(head, axis, [((i + 1) % count, i) for i in range(ends)]),
            ],
            axis=dim,
        )
    return cells


def valid_conv(padded, kernel, spread):
    out = lax.conv_general_dilated(
        padded[None],
        kernel,
        (1, 1),
        "VALID",
        rhs_dilation=(spread, spread),
        dimension_numbers=("NHWC", "HWIO", "NHWC"),
        preferred_element_type=jnp.float32,
    )
    return out[0]


def average(block_out, flipped):
    return ((block_out.astype(jnp.float32) + flipped.astype(jnp.float32)) * 0.5).astype(
        jnp.bfloat16
    )


def by_rows(contact_map, w_near, w_far):
    blocks = w_near.shape[0]
    state = lax.all_to_all(contact_map, "cols", split_axis=0, concat_axis=1, tiled=True)
    for block in range(blocks):
        padded = extended(state, ((("rows", "cols"), 0),), NEAR)
        padded = jnp.pad(padded, ((0, 0), (NEAR, NEAR), (0, 0)))
        hidden = jax.nn.relu(valid_conv(padded, w_near[block], NEAR)).astype(jnp.bfloat16)
        padded = extended(hidden, ((("rows", "cols"), 0),), FAR)
        padded = jnp.pad(padded, ((0, 0), (FAR, FAR), (0, 0)))
        block_out = (state.astype(jnp.float32) + valid_conv(padded, w_far[block], FAR)).astype(
            jnp.bfloat16
        )
        mirrored = lax.all_to_all(
            block_out, ("rows", "cols"), split_axis=1, concat_axis=0, tiled=True
        )
        state = average(block_out, jnp.swapaxes(mirrored, 0, 1))
    return lax.all_to_all(state, "cols", split_axis=1, concat_axis=0, tiled=True)


def flip(cells):
    return jnp.transpose(cells, (1, 0, 2))


def tile_kernel(
    count, side, x_ref, near_ref, far_ref, out_ref,
    pads, turned, strips, corners, mirror, hidden, near, far,
    load_sem, send_sem, recv_sem, mirror_sem,
):
    blocks, channels = near_ref.shape[0], near_ref.shape[-1]
    row, col = lax.axis_index("rows"), lax.axis_index("cols")
    last = count - 1
    inner = slice(HALO, HALO + side)
    body = slice(PAD, PAD + side)
    reach = side + 2 * FAR
    span = side + PAD

    load = pltpu.make_async_copy(x_ref, pads.at[0, inner, body], load_sem.at[0])
    load.start()

    def there(step):
        di, dj = step
        ok = []
        if di:
            ok.append(row > 0 if di < 0 else row < last)
        if dj:
            ok.append(col > 0 if dj < 0 else col < last)
        return ok[0] if len(ok) == 1 else jnp.logical_and(*ok)

    barrier = pltpu.get_barrier_semaphore()
    friends = (row != col).astype(jnp.int32)

    @pl.when(row != col)
    def _():
        pl.semaphore_signal(
            barrier, inc=1, device_id={"rows": col, "cols": row}, device_id_type=MESH
        )

    for step in SIDES:
        yes = there(step)
        friends += yes.astype(jnp.int32)

        @pl.when(yes)
        def _():
            pl.semaphore_signal(
                barrier, inc=1, device_id={"rows": row + step[0], "cols": col + step[1]},
                device_id_type=MESH,
            )

    load_near = pltpu.make_async_copy(near_ref, near, load_sem.at[1])
    load_far = pltpu.make_async_copy(far_ref, far, load_sem.at[2])
    load_near.start()
    load_far.start()

    def clear(ref):
        ref[...] = jnp.zeros(ref.shape, ref.dtype)

    def clear_off_map(ref, height, left, width):
        for at_edge, part in (
            (row == 0, (slice(0, height), slice(None))),
            (row == last, (slice(height + side, height * 2 + side), slice(None))),
            (col == 0, (slice(None), slice(left - width, left))),
            (col == last, (slice(None), slice(left + side, left + side + width))),
        ):
            pl.when(at_edge)(functools.partial(clear, ref.at[part]))

    def rim_copy(n, at):
        di, dj = SIDES[at]
        if di and dj:
            source, target = corners.at[n, 0, at], corners.at[n, 1, at]
        elif di:
            rows = slice(HALO, 2 * HALO) if di < 0 else slice(side, side + HALO)
            to = slice(HALO + side, 2 * HALO + side) if di < 0 else slice(0, HALO)
            source, target = pads.at[n, rows, body], pads.at[n, to, body]
        else:
            source = turned.at[n, 0 if dj < 0 else 1]
            target = strips.at[n, 1 if dj < 0 else 0]
        return pltpu.make_async_remote_copy(
            src_ref=source, dst_ref=target,
            send_sem=send_sem.at[n, at], recv_sem=recv_sem.at[n, at],
            device_id={"rows": row + di, "cols": col + dj}, device_id_type=MESH,
        )

    def rim_start(n, ats):
        for at in ats:
            @pl.when(there(SIDES[at]))
            def _():
                rim_copy(n, at).start()

    def rim(n, cells, head, tail):
        turned[n, 0] = head
        turned[n, 1] = tail
        rim_start(n, (0, 1))
        pads[n, inner, body] = cells
        for at in range(2, 6):
            di, dj = SIDES[at]
            rows = slice(0, HALO) if di < 0 else slice(side - HALO, side)
            bins = slice(0, PACK) if dj < 0 else slice(side - PACK, side)
            corners[n, 0, at] = cells[rows, bins].reshape(HALO * PACK, channels)
        rim_start(n, range(2, 8))

    def rim_wait(n):
        for at, (di, dj) in enumerate(SIDES):
            @pl.when(there((-di, -dj)))
            def _():
                rim_copy(n, at).wait_recv()
                if not di:
                    bins = slice(PAD - HALO, PAD) if dj > 0 else slice(
                        PAD + side, PAD + side + HALO)
                    pads[n, inner, bins] = flip(strips[n, 0 if dj > 0 else 1])
                elif dj:
                    rows = slice(0, HALO) if di > 0 else slice(HALO + side, 2 * HALO + side)
                    bins = slice(PAD - PACK, PAD) if dj > 0 else slice(
                        PAD + side, PAD + side + PACK)
                    pads[n, rows, bins] = corners[n, 1, at].reshape(HALO, PACK, channels)

    def hidden_of(n, weights):
        first, wide = PAD - HALO, weights.shape[1]
        shifted = [
            pads[n, :, first + NEAR * b:first + NEAR * b + span] for b in range(3)
        ]
        taps = [
            shifted[b][NEAR * a:NEAR * a + reach].reshape(reach * span, channels)
            for a in range(3) for b in range(3)
        ]
        total = jnp.dot(
            jnp.concatenate(taps, axis=1), weights, preferred_element_type=jnp.float32
        )
        hidden[..., :wide] = (
            jnp.maximum(total, 0.0).astype(hidden.dtype).reshape(reach, span, wide)
        )
        clear_off_map(hidden, FAR, FAR, FAR)

    def block_out_of(n, half, weights):
        lanes = slice(half * channels, (half + 1) * channels)
        shifted = [hidden[:, FAR * b:FAR * b + side, lanes] for b in range(3)]
        taps = [
            shifted[b][FAR * a:FAR * a + side].reshape(side * side, channels)
            for a in range(3) for b in range(3)
        ]
        total = jnp.dot(
            jnp.concatenate(taps, axis=1), weights, preferred_element_type=jnp.float32
        ).reshape(side, side, channels)
        return (pads[n, inner, body].astype(jnp.float32) + total).astype(jnp.bfloat16)

    def straight(w, n):
        return w[n].reshape(9 * channels, channels)

    def crossed(w, n):
        return jnp.concatenate([w[n, b, a] for a in range(3) for b in range(3)], axis=0)

    for n in range(blocks):
        clear_off_map(pads.at[n], HALO, PAD, PAD)

    load.wait()
    state = pads[0, inner, body]
    turn = flip(state)
    pl.semaphore_wait(barrier, friends)
    rim(0, state, turn[:HALO], turn[side - HALO:])
    load_near.wait()
    load_far.wait()

    for n in range(blocks):
        rim_wait(n)
        if n == 0:
            hidden_of(n, straight(near, n))
            block_out = block_out_of(n, 0, straight(far, n))
            mirror[0] = block_out
            swap = pltpu.make_async_remote_copy(
                src_ref=mirror.at[0], dst_ref=mirror.at[1],
                send_sem=mirror_sem.at[0], recv_sem=mirror_sem.at[1],
                device_id={"rows": col, "cols": row}, device_id_type=MESH,
            )

            @pl.when(row != col)
            def _():
                swap.start()

            @pl.when(row == col)
            def _():
                mirror[1] = block_out

            turn = flip(block_out)

            @pl.when(row != col)
            def _():
                swap.wait_recv()

            flipped = mirror[1]
            turn = average(turn, flipped)
            state = average(block_out, flip(flipped))
        else:
            hidden_of(n, jnp.concatenate([straight(near, n), crossed(near, n)], axis=1))
            block_out = block_out_of(n, 0, straight(far, n))
            state = average(block_out, block_out_of(n, 1, crossed(far, n)))
            turn = flip(state)
        if n < blocks - 1:
            rim(n + 1, state, turn[:HALO], turn[side - HALO:])
    out_ref[...] = state

    @pl.when(row != col)
    def _():
        swap.wait_send()

    for n in range(blocks):
        for at, step in enumerate(SIDES):
            @pl.when(there(step))
            def _():
                rim_copy(n, at).wait_send()


def by_tiles(contact_map, w_near, w_far):
    blocks, channels = w_near.shape[0], w_near.shape[-1]
    side, count = contact_map.shape[0], lax.axis_size("rows")
    kind = contact_map.dtype
    return pl.pallas_call(
        functools.partial(tile_kernel, count, side),
        out_shape=jax.ShapeDtypeStruct(contact_map.shape, kind),
        in_specs=[pl.BlockSpec(memory_space=pltpu.HBM)] * 3,
        out_specs=pl.BlockSpec(memory_space=pltpu.VMEM),
        scratch_shapes=[
            pltpu.VMEM((blocks, side + 2 * HALO, side + 2 * PAD, channels), kind),
            pltpu.VMEM((blocks, 2, HALO, side, channels), kind),
            pltpu.VMEM((blocks, 2, HALO, side, channels), kind),
            pltpu.VMEM((blocks, 2, len(SIDES), HALO * PACK, channels), kind),
            pltpu.VMEM((2, side, side, channels), kind),
            pltpu.VMEM((side + 2 * FAR, side + PAD, 2 * channels), kind),
            pltpu.VMEM(w_near.shape, kind),
            pltpu.VMEM(w_far.shape, kind),
            pltpu.SemaphoreType.DMA((3,)),
            pltpu.SemaphoreType.DMA((blocks, len(SIDES))),
            pltpu.SemaphoreType.DMA((blocks, len(SIDES))),
            pltpu.SemaphoreType.DMA((2,)),
        ],
        compiler_params=pltpu.CompilerParams(
            collective_id=0, has_side_effects=True, vmem_limit_bytes=64 * 2**20
        ),
    )(contact_map, w_near, w_far)


def on_device(contact_map, w_near, w_far):
    side = contact_map.shape[0]
    square = side == contact_map.shape[1] and side % PAD == 0
    if square and lax.axis_size("rows") == lax.axis_size("cols") and w_near.shape[0] > 1:
        return by_tiles(contact_map, w_near, w_far)
    return by_rows(contact_map, w_near, w_far)


def solution(mesh):
    in_specs = (P(("groups", "rows"), "cols", None), P(), P())
    out_specs = P(("groups", "rows"), "cols", None)
    return jax.shard_map(
        on_device, mesh=mesh, in_specs=in_specs, out_specs=out_specs, check_vma=False
    )
```

```python
import functools

import jax
import jax.numpy as jnp
from jax import lax
from jax.experimental import pallas as pl
from jax.experimental.pallas import tpu as pltpu
from jax.sharding import PartitionSpec as P

MESH = pl.DeviceIdType.MESH
NEAR, FAR = 2, 4
HALO = NEAR + FAR
PAD, PACK = 16, 8
SIDES = [(-1, 0), (1, 0), (0, -1), (0, 1), (-1, -1), (-1, 1), (1, -1), (1, 1)]


def extended(cells, sides, width):
    for axis, dim in sides:
        count = lax.axis_size(axis)
        ends = count - 1
        head = lax.slice_in_dim(cells, 0, width, axis=dim)
        tail = lax.slice_in_dim(cells, cells.shape[dim] - width, cells.shape[dim], axis=dim)
        cells = jnp.concatenate(
            [
                lax.ppermute(tail, axis, [(i, (i + 1) % count) for i in range(ends)]),
                cells,
                lax.ppermute(head, axis, [((i + 1) % count, i) for i in range(ends)]),
            ],
            axis=dim,
        )
    return cells


def valid_conv(padded, kernel, spread):
    out = lax.conv_general_dilated(
        padded[None],
        kernel,
        (1, 1),
        "VALID",
        rhs_dilation=(spread, spread),
        dimension_numbers=("NHWC", "HWIO", "NHWC"),
        preferred_element_type=jnp.float32,
    )
    return out[0]


def average(block_out, flipped):
    return ((block_out.astype(jnp.float32) + flipped.astype(jnp.float32)) * 0.5).astype(
        jnp.bfloat16
    )


def by_rows(contact_map, w_near, w_far):
    blocks = w_near.shape[0]
    state = lax.all_to_all(contact_map, "cols", split_axis=0, concat_axis=1, tiled=True)
    for block in range(blocks):
        padded = extended(state, ((("rows", "cols"), 0),), NEAR)
        padded = jnp.pad(padded, ((0, 0), (NEAR, NEAR), (0, 0)))
        hidden = jax.nn.relu(valid_conv(padded, w_near[block], NEAR)).astype(jnp.bfloat16)
        padded = extended(hidden, ((("rows", "cols"), 0),), FAR)
        padded = jnp.pad(padded, ((0, 0), (FAR, FAR), (0, 0)))
        block_out = (state.astype(jnp.float32) + valid_conv(padded, w_far[block], FAR)).astype(
            jnp.bfloat16
        )
        mirrored = lax.all_to_all(
            block_out, ("rows", "cols"), split_axis=1, concat_axis=0, tiled=True
        )
        state = average(block_out, jnp.swapaxes(mirrored, 0, 1))
    return lax.all_to_all(state, "cols", split_axis=1, concat_axis=0, tiled=True)


def flip(cells):
    return jnp.transpose(cells, (1, 0, 2))


def tile_kernel(
    count, side, x_ref, near_ref, far_ref, out_ref,
    pads, turned, strips, corners, mirror, hidden, near, far,
    load_sem, send_sem, recv_sem, mirror_sem,
):
    blocks, channels = near_ref.shape[0], near_ref.shape[-1]
    row, col = lax.axis_index("rows"), lax.axis_index("cols")
    last = count - 1
    inner = slice(HALO, HALO + side)
    body = slice(PAD, PAD + side)
    reach = side + 2 * FAR
    span = side + PAD

    load = pltpu.make_async_copy(x_ref, pads.at[0, inner, body], load_sem.at[0])
    load.start()

    def there(step):
        di, dj = step
        ok = []
        if di:
            ok.append(row > 0 if di < 0 else row < last)
        if dj:
            ok.append(col > 0 if dj < 0 else col < last)
        return ok[0] if len(ok) == 1 else jnp.logical_and(*ok)

    barrier = pltpu.get_barrier_semaphore()
    friends = (row != col).astype(jnp.int32)

    @pl.when(row != col)
    def _():
        pl.semaphore_signal(
            barrier, inc=1, device_id={"rows": col, "cols": row}, device_id_type=MESH
        )

    for step in SIDES:
        yes = there(step)
        friends += yes.astype(jnp.int32)

        @pl.when(yes)
        def _():
            pl.semaphore_signal(
                barrier, inc=1, device_id={"rows": row + step[0], "cols": col + step[1]},
                device_id_type=MESH,
            )

    load_near = pltpu.make_async_copy(near_ref, near, load_sem.at[1])
    load_far = pltpu.make_async_copy(far_ref, far, load_sem.at[2])
    load_near.start()
    load_far.start()

    def clear(ref):
        ref[...] = jnp.zeros(ref.shape, ref.dtype)

    def clear_off_map(ref, height, left, width):
        for at_edge, part in (
            (row == 0, (slice(0, height), slice(None))),
            (row == last, (slice(height + side, height * 2 + side), slice(None))),
            (col == 0, (slice(None), slice(left - width, left))),
            (col == last, (slice(None), slice(left + side, left + side + width))),
        ):
            pl.when(at_edge)(functools.partial(clear, ref.at[part]))

    def rim_copy(n, at):
        di, dj = SIDES[at]
        if di and dj:
            source, target = corners.at[n, 0, at], corners.at[n, 1, at]
        elif di:
            rows = slice(HALO, 2 * HALO) if di < 0 else slice(side, side + HALO)
            to = slice(HALO + side, 2 * HALO + side) if di < 0 else slice(0, HALO)
            source, target = pads.at[n, rows, body], pads.at[n, to, body]
        else:
            source = turned.at[n, 0 if dj < 0 else 1]
            target = strips.at[n, 1 if dj < 0 else 0]
        return pltpu.make_async_remote_copy(
            src_ref=source, dst_ref=target,
            send_sem=send_sem.at[n, at], recv_sem=recv_sem.at[n, at],
            device_id={"rows": row + di, "cols": col + dj}, device_id_type=MESH,
        )

    def rim_start(n, ats):
        for at in ats:
            @pl.when(there(SIDES[at]))
            def _():
                rim_copy(n, at).start()

    def send_columns(n, end, turn):
        turned[n, end] = turn[:HALO] if end == 0 else turn[turn.shape[0] - HALO:]
        rim_start(n, (2 + end,))

    def send_rows(n, cells):
        rim_start(n, (0, 1))
        for at in range(4, 8):
            di, dj = SIDES[at]
            rows = slice(0, HALO) if di < 0 else slice(side - HALO, side)
            bins = slice(0, PACK) if dj < 0 else slice(side - PACK, side)
            corners[n, 0, at] = cells[rows, bins].reshape(HALO * PACK, channels)
        rim_start(n, range(4, 8))

    def rim_wait(n):
        for at, (di, dj) in enumerate(SIDES):
            @pl.when(there((-di, -dj)))
            def _():
                rim_copy(n, at).wait_recv()
                if not di:
                    bins = slice(PAD - HALO, PAD) if dj > 0 else slice(
                        PAD + side, PAD + side + HALO)
                    pads[n, inner, bins] = flip(strips[n, 0 if dj > 0 else 1])
                elif dj:
                    rows = slice(0, HALO) if di > 0 else slice(HALO + side, 2 * HALO + side)
                    bins = slice(PAD - PACK, PAD) if dj > 0 else slice(
                        PAD + side, PAD + side + PACK)
                    pads[n, rows, bins] = corners[n, 1, at].reshape(HALO, PACK, channels)

    def hidden_of(n, weights):
        first, wide = PAD - HALO, weights.shape[1]
        shifted = [
            pads[n, :, first + NEAR * b:first + NEAR * b + span] for b in range(3)
        ]
        taps = [
            shifted[b][NEAR * a:NEAR * a + reach].reshape(reach * span, channels)
            for a in range(3) for b in range(3)
        ]
        total = jnp.dot(
            jnp.concatenate(taps, axis=1), weights, preferred_element_type=jnp.float32
        )
        hidden[..., :wide] = (
            jnp.maximum(total, 0.0).astype(hidden.dtype).reshape(reach, span, wide)
        )
        clear_off_map(hidden, FAR, FAR, FAR)

    def block_out_of(n, half, weights, rows):
        lanes = slice(half * channels, (half + 1) * channels)
        start, size = rows.start, rows.stop - rows.start
        shifted = [
            hidden[start:rows.stop + 2 * FAR, FAR * b:FAR * b + side, lanes] for b in range(3)
        ]
        taps = [
            shifted[b][FAR * a:FAR * a + size].reshape(size * side, channels)
            for a in range(3) for b in range(3)
        ]
        total = jnp.dot(
            jnp.concatenate(taps, axis=1), weights, preferred_element_type=jnp.float32
        ).reshape(size, side, channels)
        own = pads[n, HALO + start:HALO + rows.stop, body]
        return (own.astype(jnp.float32) + total).astype(jnp.bfloat16)

    def straight(w, n):
        return w[n].reshape(9 * channels, channels)

    def crossed(w, n):
        return jnp.concatenate([w[n, b, a] for a in range(3) for b in range(3)], axis=0)

    for n in range(blocks):
        clear_off_map(pads.at[n], HALO, PAD, PAD)

    halves = [slice(0, side // 2), slice(side // 2, side)]
    whole = slice(0, side)
    swaps = [
        pltpu.make_async_remote_copy(
            src_ref=mirror.at[0, part], dst_ref=mirror.at[1, part],
            send_sem=mirror_sem.at[0, k], recv_sem=mirror_sem.at[1, k],
            device_id={"rows": col, "cols": row}, device_id_type=MESH,
        )
        for k, part in enumerate(halves)
    ]

    load.wait()
    pl.semaphore_wait(barrier, friends)
    state = pads[0, inner, body]
    send_rows(0, state)
    turn = flip(state)
    send_columns(0, 0, turn)
    send_columns(0, 1, turn)
    load_near.wait()
    load_far.wait()

    for n in range(blocks):
        rim_wait(n)
        if n == 0:
            hidden_of(n, straight(near, n))
            for swap, part in zip(swaps, halves):
                mirror[0, part] = block_out_of(n, 0, straight(far, n), part)

                @pl.when(row != col)
                def _():
                    swap.start()

                @pl.when(row == col)
                def _():
                    mirror[1, part] = mirror[0, part]

            block_out = mirror[0]
            turn = flip(block_out)
            for end, (swap, part) in enumerate(zip(swaps, halves)):
                @pl.when(row != col)
                def _():
                    swap.wait_recv()

                send_columns(n + 1, end, average(turn[part], mirror[1, part]))
            state = average(block_out, flip(mirror[1]))
            pads[n + 1, inner, body] = state
            send_rows(n + 1, state)
        else:
            hidden_of(n, jnp.concatenate([straight(near, n), crossed(near, n)], axis=1))
            state = average(
                block_out_of(n, 0, straight(far, n), whole),
                block_out_of(n, 1, crossed(far, n), whole),
            )
            if n < blocks - 1:
                pads[n + 1, inner, body] = state
                send_rows(n + 1, state)
                turn = flip(state)
                send_columns(n + 1, 0, turn)
                send_columns(n + 1, 1, turn)
    out_ref[...] = state

    @pl.when(row != col)
    def _():
        for swap in swaps:
            swap.wait_send()

    for n in range(blocks):
        for at, step in enumerate(SIDES):
            @pl.when(there(step))
            def _():
                rim_copy(n, at).wait_send()


def by_tiles(contact_map, w_near, w_far):
    blocks, channels = w_near.shape[0], w_near.shape[-1]
    side, count = contact_map.shape[0], lax.axis_size("rows")
    kind = contact_map.dtype
    return pl.pallas_call(
        functools.partial(tile_kernel, count, side),
        out_shape=jax.ShapeDtypeStruct(contact_map.shape, kind),
        in_specs=[pl.BlockSpec(memory_space=pltpu.HBM)] * 3,
        out_specs=pl.BlockSpec(memory_space=pltpu.VMEM),
        scratch_shapes=[
            pltpu.VMEM((blocks, side + 2 * HALO, side + 2 * PAD, channels), kind),
            pltpu.VMEM((blocks, 2, HALO, side, channels), kind),
            pltpu.VMEM((blocks, 2, HALO, side, channels), kind),
            pltpu.VMEM((blocks, 2, len(SIDES), HALO * PACK, channels), kind),
            pltpu.VMEM((2, side, side, channels), kind),
            pltpu.VMEM((side + 2 * FAR, side + PAD, 2 * channels), kind),
            pltpu.VMEM(w_near.shape, kind),
            pltpu.VMEM(w_far.shape, kind),
            pltpu.SemaphoreType.DMA((3,)),
            pltpu.SemaphoreType.DMA((blocks, len(SIDES))),
            pltpu.SemaphoreType.DMA((blocks, len(SIDES))),
            pltpu.SemaphoreType.DMA((2, 2)),
        ],
        compiler_params=pltpu.CompilerParams(
            collective_id=0, has_side_effects=True, vmem_limit_bytes=107 * 2**19
        ),
    )(contact_map, w_near, w_far)


def on_device(contact_map, w_near, w_far):
    side = contact_map.shape[0]
    square = side == contact_map.shape[1] and side % PAD == 0
    if square and lax.axis_size("rows") == lax.axis_size("cols") and w_near.shape[0] > 1:
        return by_tiles(contact_map, w_near, w_far)
    return by_rows(contact_map, w_near, w_far)


def solution(mesh):
    in_specs = (P(("groups", "rows"), "cols", None), P(), P())
    out_specs = P(("groups", "rows"), "cols", None)
    return jax.shard_map(
        on_device, mesh=mesh, in_specs=in_specs, out_specs=out_specs, check_vma=False
    )
```

```python
import functools

import jax
import jax.numpy as jnp
from jax import lax
from jax.experimental import pallas as pl
from jax.experimental.pallas import tpu as pltpu
from jax.sharding import PartitionSpec as P

MESH = pl.DeviceIdType.MESH
NEAR, FAR = 2, 4
HALO = NEAR + FAR
PAD, PACK = 16, 8
SIDES = [(-1, 0), (1, 0), (0, -1), (0, 1), (-1, -1), (-1, 1), (1, -1), (1, 1)]


def extended(cells, sides, width):
    for axis, dim in sides:
        count = lax.axis_size(axis)
        ends = count - 1
        head = lax.slice_in_dim(cells, 0, width, axis=dim)
        tail = lax.slice_in_dim(cells, cells.shape[dim] - width, cells.shape[dim], axis=dim)
        cells = jnp.concatenate(
            [
                lax.ppermute(tail, axis, [(i, (i + 1) % count) for i in range(ends)]),
                cells,
                lax.ppermute(head, axis, [((i + 1) % count, i) for i in range(ends)]),
            ],
            axis=dim,
        )
    return cells


def valid_conv(padded, kernel, spread):
    out = lax.conv_general_dilated(
        padded[None],
        kernel,
        (1, 1),
        "VALID",
        rhs_dilation=(spread, spread),
        dimension_numbers=("NHWC", "HWIO", "NHWC"),
        preferred_element_type=jnp.float32,
    )
    return out[0]


def average(block_out, flipped):
    return ((block_out.astype(jnp.float32) + flipped.astype(jnp.float32)) * 0.5).astype(
        jnp.bfloat16
    )


def by_rows(contact_map, w_near, w_far):
    blocks = w_near.shape[0]
    state = lax.all_to_all(contact_map, "cols", split_axis=0, concat_axis=1, tiled=True)
    for block in range(blocks):
        padded = extended(state, ((("rows", "cols"), 0),), NEAR)
        padded = jnp.pad(padded, ((0, 0), (NEAR, NEAR), (0, 0)))
        hidden = jax.nn.relu(valid_conv(padded, w_near[block], NEAR)).astype(jnp.bfloat16)
        padded = extended(hidden, ((("rows", "cols"), 0),), FAR)
        padded = jnp.pad(padded, ((0, 0), (FAR, FAR), (0, 0)))
        block_out = (state.astype(jnp.float32) + valid_conv(padded, w_far[block], FAR)).astype(
            jnp.bfloat16
        )
        mirrored = lax.all_to_all(
            block_out, ("rows", "cols"), split_axis=1, concat_axis=0, tiled=True
        )
        state = average(block_out, jnp.swapaxes(mirrored, 0, 1))
    return lax.all_to_all(state, "cols", split_axis=1, concat_axis=0, tiled=True)


def flip(cells):
    return jnp.transpose(cells, (1, 0, 2))


def tile_kernel(
    count, side, x_ref, near_ref, far_ref, out_ref,
    pads, turned, strips, corners, mirror, hidden, near, far,
    load_sem, send_sem, recv_sem, mirror_sem,
):
    blocks, channels = near_ref.shape[0], near_ref.shape[-1]
    row, col = lax.axis_index("rows"), lax.axis_index("cols")
    last = count - 1
    inner = slice(HALO, HALO + side)
    body = slice(PAD, PAD + side)
    reach = side + 2 * FAR
    span = side + PAD

    load = pltpu.make_async_copy(x_ref, pads.at[0, inner, body], load_sem.at[0])
    load.start()

    def there(step):
        di, dj = step
        ok = []
        if di:
            ok.append(row > 0 if di < 0 else row < last)
        if dj:
            ok.append(col > 0 if dj < 0 else col < last)
        return ok[0] if len(ok) == 1 else jnp.logical_and(*ok)

    barrier = pltpu.get_barrier_semaphore()
    friends = (row != col).astype(jnp.int32)

    @pl.when(row != col)
    def _():
        pl.semaphore_signal(
            barrier, inc=1, device_id={"rows": col, "cols": row}, device_id_type=MESH
        )

    for step in SIDES:
        yes = there(step)
        friends += yes.astype(jnp.int32)

        @pl.when(yes)
        def _():
            pl.semaphore_signal(
                barrier, inc=1, device_id={"rows": row + step[0], "cols": col + step[1]},
                device_id_type=MESH,
            )

    load_near = pltpu.make_async_copy(near_ref, near, load_sem.at[1])
    load_far = pltpu.make_async_copy(far_ref, far, load_sem.at[2])
    load_near.start()
    load_far.start()

    def clear(ref):
        ref[...] = jnp.zeros(ref.shape, ref.dtype)

    def clear_off_map(ref, height, left, width):
        for at_edge, part in (
            (row == 0, (slice(0, height), slice(None))),
            (row == last, (slice(height + side, height * 2 + side), slice(None))),
            (col == 0, (slice(None), slice(left - width, left))),
            (col == last, (slice(None), slice(left + side, left + side + width))),
        ):
            pl.when(at_edge)(functools.partial(clear, ref.at[part]))

    def rim_copy(n, at):
        di, dj = SIDES[at]
        if di and dj:
            source, target = corners.at[n, 0, at], corners.at[n, 1, at]
        elif di:
            rows = slice(HALO, 2 * HALO) if di < 0 else slice(side, side + HALO)
            to = slice(HALO + side, 2 * HALO + side) if di < 0 else slice(0, HALO)
            source, target = pads.at[n, rows, body], pads.at[n, to, body]
        else:
            source = turned.at[n, 0 if dj < 0 else 1]
            target = strips.at[n, 1 if dj < 0 else 0]
        return pltpu.make_async_remote_copy(
            src_ref=source, dst_ref=target,
            send_sem=send_sem.at[n, at], recv_sem=recv_sem.at[n, at],
            device_id={"rows": row + di, "cols": col + dj}, device_id_type=MESH,
        )

    def rim_start(n, ats):
        for at in ats:
            @pl.when(there(SIDES[at]))
            def _():
                rim_copy(n, at).start()

    def send_columns(n, end, turn):
        turned[n, end] = turn[:HALO] if end == 0 else turn[turn.shape[0] - HALO:]
        rim_start(n, (2 + end,))

    def send_rows(n):
        rim_start(n, (0, 1))

    def send_corners(n, cells):
        for at in range(4, 8):
            di, dj = SIDES[at]
            rows = slice(0, HALO) if di < 0 else slice(side - HALO, side)
            bins = slice(0, PACK) if dj < 0 else slice(side - PACK, side)
            corners[n, 0, at] = cells[rows, bins].reshape(HALO * PACK, channels)
        rim_start(n, range(4, 8))

    def rim_wait(n, which):
        for at, (di, dj) in enumerate(SIDES):
            if di != which:
                continue

            @pl.when(there((-di, -dj)))
            def _():
                rim_copy(n, at).wait_recv()
                if not di:
                    bins = slice(PAD - HALO, PAD) if dj > 0 else slice(
                        PAD + side, PAD + side + HALO)
                    pads[n, inner, bins] = flip(strips[n, 0 if dj > 0 else 1])
                elif dj:
                    rows = slice(0, HALO) if di > 0 else slice(HALO + side, 2 * HALO + side)
                    bins = slice(PAD - PACK, PAD) if dj > 0 else slice(
                        PAD + side, PAD + side + PACK)
                    pads[n, rows, bins] = corners[n, 1, at].reshape(HALO, PACK, channels)

    def hidden_rows(n, weights, start, size):
        first, wide = PAD - HALO, weights.shape[1]
        shifted = [
            pads[n, pl.ds(start, size + 2 * NEAR), first + NEAR * b:first + NEAR * b + span]
            for b in range(3)
        ]
        taps = [
            shifted[b][NEAR * a:NEAR * a + size].reshape(size * span, channels)
            for a in range(3) for b in range(3)
        ]
        total = jnp.dot(
            jnp.concatenate(taps, axis=1), weights, preferred_element_type=jnp.float32
        )
        hidden[pl.ds(start, size), :, :wide] = (
            jnp.maximum(total, 0.0).astype(hidden.dtype).reshape(size, span, wide)
        )

    def hidden_of(n, weights):
        rim_wait(n, 0)
        hidden_rows(n, weights, HALO, side - 2 * NEAR)
        odd = lax.rem(row, 2)
        for k in range(2):
            above = odd == 1 - k
            pl.when(above)(functools.partial(rim_wait, n, 1))
            pl.when(jnp.logical_not(above))(functools.partial(rim_wait, n, -1))
            hidden_rows(n, weights, jnp.where(above, 0, reach - HALO), HALO)
        clear_off_map(hidden, FAR, FAR, FAR)

    def block_out_of(n, half, weights, rows):
        lanes = slice(half * channels, (half + 1) * channels)
        start, size = rows.start, rows.stop - rows.start
        shifted = [
            hidden[start:rows.stop + 2 * FAR, FAR * b:FAR * b + side, lanes] for b in range(3)
        ]
        taps = [
            shifted[b][FAR * a:FAR * a + size].reshape(size * side, channels)
            for a in range(3) for b in range(3)
        ]
        total = jnp.dot(
            jnp.concatenate(taps, axis=1), weights, preferred_element_type=jnp.float32
        ).reshape(size, side, channels)
        own = pads[n, HALO + start:HALO + rows.stop, body]
        return (own.astype(jnp.float32) + total).astype(jnp.bfloat16)

    def straight(w, n):
        return w[n].reshape(9 * channels, channels)

    def crossed(w, n):
        return jnp.concatenate([w[n, b, a] for a in range(3) for b in range(3)], axis=0)

    for n in range(blocks):
        clear_off_map(pads.at[n], HALO, PAD, PAD)

    halves = [slice(0, side // 2), slice(side // 2, side)]
    whole = slice(0, side)
    swaps = [
        pltpu.make_async_remote_copy(
            src_ref=mirror.at[0, part], dst_ref=mirror.at[1, part],
            send_sem=mirror_sem.at[0, k], recv_sem=mirror_sem.at[1, k],
            device_id={"rows": col, "cols": row}, device_id_type=MESH,
        )
        for k, part in enumerate(halves)
    ]

    load.wait()
    pl.semaphore_wait(barrier, friends)
    send_rows(0)
    state = pads[0, inner, body]
    turn = flip(state)
    send_columns(0, 0, turn)
    send_columns(0, 1, turn)
    send_corners(0, state)
    load_near.wait()
    load_far.wait()

    for n in range(blocks):
        if n == 0:
            hidden_of(n, straight(near, n))
            for swap, part in zip(swaps, halves):
                mirror[0, part] = block_out_of(n, 0, straight(far, n), part)

                @pl.when(row != col)
                def _():
                    swap.start()

                @pl.when(row == col)
                def _():
                    mirror[1, part] = mirror[0, part]

            block_out = mirror[0]
            turn = flip(block_out)
            for end, (swap, part) in enumerate(zip(swaps, halves)):
                @pl.when(row != col)
                def _():
                    swap.wait_recv()

                send_columns(n + 1, end, average(turn[part], mirror[1, part]))
            state = average(block_out, flip(mirror[1]))
            pads[n + 1, inner, body] = state
            send_rows(n + 1)
            send_corners(n + 1, state)
        else:
            hidden_of(n, jnp.concatenate([straight(near, n), crossed(near, n)], axis=1))
            state = average(
                block_out_of(n, 0, straight(far, n), whole),
                block_out_of(n, 1, crossed(far, n), whole),
            )
            if n < blocks - 1:
                pads[n + 1, inner, body] = state
                turn = flip(state)
                send_columns(n + 1, 0, turn)
                send_columns(n + 1, 1, turn)
                send_rows(n + 1)
                send_corners(n + 1, state)
    out_ref[...] = state

    @pl.when(row != col)
    def _():
        for swap in swaps:
            swap.wait_send()

    for n in range(blocks):
        for at, step in enumerate(SIDES):
            @pl.when(there(step))
            def _():
                rim_copy(n, at).wait_send()


def by_tiles(contact_map, w_near, w_far):
    blocks, channels = w_near.shape[0], w_near.shape[-1]
    side, count = contact_map.shape[0], lax.axis_size("rows")
    kind = contact_map.dtype
    return pl.pallas_call(
        functools.partial(tile_kernel, count, side),
        out_shape=jax.ShapeDtypeStruct(contact_map.shape, kind),
        in_specs=[pl.BlockSpec(memory_space=pltpu.HBM)] * 3,
        out_specs=pl.BlockSpec(memory_space=pltpu.VMEM),
        scratch_shapes=[
            pltpu.VMEM((blocks, side + 2 * HALO, side + 2 * PAD, channels), kind),
            pltpu.VMEM((blocks, 2, HALO, side, channels), kind),
            pltpu.VMEM((blocks, 2, HALO, side, channels), kind),
            pltpu.VMEM((blocks, 2, len(SIDES), HALO * PACK, channels), kind),
            pltpu.VMEM((2, side, side, channels), kind),
            pltpu.VMEM((side + 2 * FAR, side + PAD, 2 * channels), kind),
            pltpu.VMEM(w_near.shape, kind),
            pltpu.VMEM(w_far.shape, kind),
            pltpu.SemaphoreType.DMA((3,)),
            pltpu.SemaphoreType.DMA((blocks, len(SIDES))),
            pltpu.SemaphoreType.DMA((blocks, len(SIDES))),
            pltpu.SemaphoreType.DMA((2, 2)),
        ],
        compiler_params=pltpu.CompilerParams(
            collective_id=0, has_side_effects=True, vmem_limit_bytes=107 * 2**19
        ),
    )(contact_map, w_near, w_far)


def on_device(contact_map, w_near, w_far):
    side = contact_map.shape[0]
    square = side == contact_map.shape[1] and side % PAD == 0
    if square and lax.axis_size("rows") == lax.axis_size("cols") and w_near.shape[0] > 1:
        return by_tiles(contact_map, w_near, w_far)
    return by_rows(contact_map, w_near, w_far)


def solution(mesh):
    in_specs = (P(("groups", "rows"), "cols", None), P(), P())
    out_specs = P(("groups", "rows"), "cols", None)
    return jax.shard_map(
        on_device, mesh=mesh, in_specs=in_specs, out_specs=out_specs, check_vma=False
    )
```

```python
import functools

import jax
import jax.numpy as jnp
from jax import lax
from jax.experimental import pallas as pl
from jax.experimental.pallas import tpu as pltpu
from jax.sharding import PartitionSpec as P

MESH = pl.DeviceIdType.MESH
NEAR, FAR = 2, 4
HALO = NEAR + FAR
PAD, PACK = 16, 8
SIDES = [(-1, 0), (1, 0), (0, -1), (0, 1), (-1, -1), (-1, 1), (1, -1), (1, 1)]


def extended(cells, sides, width):
    for axis, dim in sides:
        count = lax.axis_size(axis)
        ends = count - 1
        head = lax.slice_in_dim(cells, 0, width, axis=dim)
        tail = lax.slice_in_dim(cells, cells.shape[dim] - width, cells.shape[dim], axis=dim)
        cells = jnp.concatenate(
            [
                lax.ppermute(tail, axis, [(i, (i + 1) % count) for i in range(ends)]),
                cells,
                lax.ppermute(head, axis, [((i + 1) % count, i) for i in range(ends)]),
            ],
            axis=dim,
        )
    return cells


def valid_conv(padded, kernel, spread):
    out = lax.conv_general_dilated(
        padded[None],
        kernel,
        (1, 1),
        "VALID",
        rhs_dilation=(spread, spread),
        dimension_numbers=("NHWC", "HWIO", "NHWC"),
        preferred_element_type=jnp.float32,
    )
    return out[0]


def average(block_out, flipped):
    return ((block_out.astype(jnp.float32) + flipped.astype(jnp.float32)) * 0.5).astype(
        jnp.bfloat16
    )


def by_rows(contact_map, w_near, w_far):
    blocks = w_near.shape[0]
    state = lax.all_to_all(contact_map, "cols", split_axis=0, concat_axis=1, tiled=True)
    for block in range(blocks):
        padded = extended(state, ((("rows", "cols"), 0),), NEAR)
        padded = jnp.pad(padded, ((0, 0), (NEAR, NEAR), (0, 0)))
        hidden = jax.nn.relu(valid_conv(padded, w_near[block], NEAR)).astype(jnp.bfloat16)
        padded = extended(hidden, ((("rows", "cols"), 0),), FAR)
        padded = jnp.pad(padded, ((0, 0), (FAR, FAR), (0, 0)))
        block_out = (state.astype(jnp.float32) + valid_conv(padded, w_far[block], FAR)).astype(
            jnp.bfloat16
        )
        mirrored = lax.all_to_all(
            block_out, ("rows", "cols"), split_axis=1, concat_axis=0, tiled=True
        )
        state = average(block_out, jnp.swapaxes(mirrored, 0, 1))
    return lax.all_to_all(state, "cols", split_axis=1, concat_axis=0, tiled=True)


def flip(cells):
    return jnp.transpose(cells, (1, 0, 2))


def tile_kernel(
    count, side, x_ref, near_ref, far_ref, out_ref,
    pads, turned, strips, corners, mirror, hidden, near, far,
    load_sem, send_sem, recv_sem, mirror_sem,
):
    blocks, channels = near_ref.shape[0], near_ref.shape[-1]
    row, col = lax.axis_index("rows"), lax.axis_index("cols")
    last = count - 1
    inner = slice(HALO, HALO + side)
    body = slice(PAD, PAD + side)
    reach = side + 2 * FAR
    span = side + PAD
    half = side // 2

    load = pltpu.make_async_copy(x_ref, pads.at[0, inner, body], load_sem.at[0])
    load.start()

    def there(step):
        di, dj = step
        ok = []
        if di:
            ok.append(row > 0 if di < 0 else row < last)
        if dj:
            ok.append(col > 0 if dj < 0 else col < last)
        return ok[0] if len(ok) == 1 else jnp.logical_and(*ok)

    barrier = pltpu.get_barrier_semaphore()
    friends = (row != col).astype(jnp.int32)

    @pl.when(row != col)
    def _():
        pl.semaphore_signal(
            barrier, inc=1, device_id={"rows": col, "cols": row}, device_id_type=MESH
        )

    for step in SIDES:
        yes = there(step)
        friends += yes.astype(jnp.int32)

        @pl.when(yes)
        def _():
            pl.semaphore_signal(
                barrier, inc=1, device_id={"rows": row + step[0], "cols": col + step[1]},
                device_id_type=MESH,
            )

    load_near = pltpu.make_async_copy(near_ref, near, load_sem.at[1])
    load_far = pltpu.make_async_copy(far_ref, far, load_sem.at[2])
    load_near.start()
    load_far.start()

    def clear(ref):
        ref[...] = jnp.zeros(ref.shape, ref.dtype)

    def clear_off_map(ref, height, left, width):
        for at_edge, part in (
            (row == 0, (slice(0, height), slice(None))),
            (row == last, (slice(height + side, height * 2 + side), slice(None))),
            (col == 0, (slice(None), slice(left - width, left))),
            (col == last, (slice(None), slice(left + side, left + side + width))),
        ):
            pl.when(at_edge)(functools.partial(clear, ref.at[part]))

    def rim_copy(n, at):
        di, dj = SIDES[at]
        if di and dj:
            source, target = corners.at[n, 0, at], corners.at[n, 1, at]
        elif di:
            rows = slice(HALO, 2 * HALO) if di < 0 else slice(side, side + HALO)
            to = slice(HALO + side, 2 * HALO + side) if di < 0 else slice(0, HALO)
            source, target = pads.at[n, rows, body], pads.at[n, to, body]
        else:
            source = turned.at[n, 0 if dj < 0 else 1]
            target = strips.at[n, 1 if dj < 0 else 0]
        return pltpu.make_async_remote_copy(
            src_ref=source, dst_ref=target,
            send_sem=send_sem.at[n, at], recv_sem=recv_sem.at[n, at],
            device_id={"rows": row + di, "cols": col + dj}, device_id_type=MESH,
        )

    def rim_start(n, ats):
        for at in ats:
            @pl.when(there(SIDES[at]))
            def _():
                rim_copy(n, at).start()

    def send_columns(n, end, turn):
        turned[n, end] = turn[:HALO] if end == 0 else turn[turn.shape[0] - HALO:]
        rim_start(n, (2 + end,))

    def send_rows(n):
        rim_start(n, (0, 1))

    def send_corners(n, cells):
        for at in range(4, 8):
            di, dj = SIDES[at]
            rows = slice(0, HALO) if di < 0 else slice(side - HALO, side)
            bins = slice(0, PACK) if dj < 0 else slice(side - PACK, side)
            corners[n, 0, at] = cells[rows, bins].reshape(HALO * PACK, channels)
        rim_start(n, range(4, 8))

    def rim_wait(n, which):
        for at, (di, dj) in enumerate(SIDES):
            if di != which:
                continue

            @pl.when(there((-di, -dj)))
            def _():
                rim_copy(n, at).wait_recv()
                if not di:
                    bins = slice(PAD - HALO, PAD) if dj > 0 else slice(
                        PAD + side, PAD + side + HALO)
                    pads[n, inner, bins] = flip(strips[n, 0 if dj > 0 else 1])
                elif dj:
                    rows = slice(0, HALO) if di > 0 else slice(HALO + side, 2 * HALO + side)
                    bins = slice(PAD - PACK, PAD) if dj > 0 else slice(
                        PAD + side, PAD + side + PACK)
                    pads[n, rows, bins] = corners[n, 1, at].reshape(HALO, PACK, channels)

    def hidden_rows(n, weights, start, size):
        first, wide = PAD - HALO, weights.shape[1]
        shifted = [
            pads[n, pl.ds(start, size + 2 * NEAR), first + NEAR * b:first + NEAR * b + span]
            for b in range(3)
        ]
        taps = [
            shifted[b][NEAR * a:NEAR * a + size].reshape(size * span, channels)
            for a in range(3) for b in range(3)
        ]
        total = jnp.dot(
            jnp.concatenate(taps, axis=1), weights, preferred_element_type=jnp.float32
        )
        hidden[pl.ds(start, size), :, :wide] = (
            jnp.maximum(total, 0.0).astype(hidden.dtype).reshape(size, span, wide)
        )

    def block_out_of(n, lane, weights, start):
        lanes = slice(lane * channels, (lane + 1) * channels)
        shifted = [
            hidden[pl.ds(start, half + 2 * FAR), FAR * b:FAR * b + side, lanes]
            for b in range(3)
        ]
        taps = [
            shifted[b][FAR * a:FAR * a + half].reshape(half * side, channels)
            for a in range(3) for b in range(3)
        ]
        total = jnp.dot(
            jnp.concatenate(taps, axis=1), weights, preferred_element_type=jnp.float32
        ).reshape(half, side, channels)
        own = pads[n, pl.ds(HALO + start, half), body]
        return (own.astype(jnp.float32) + total).astype(jnp.bfloat16)

    def halves_of(n, weights, half_done):
        rim_wait(n, 0)
        hidden_rows(n, weights, HALO, side - 2 * NEAR)
        for k in range(2):
            above = lax.rem(row, 2) == 1 - k
            pl.when(above)(functools.partial(rim_wait, n, 1))
            pl.when(jnp.logical_not(above))(functools.partial(rim_wait, n, -1))
            hidden_rows(n, weights, jnp.where(above, 0, reach - HALO), HALO)
            clear_off_map(hidden, FAR, FAR, FAR)
            half_done(k, jnp.where(above, 0, half))

    def straight(w, n):
        return w[n].reshape(9 * channels, channels)

    def crossed(w, n):
        return jnp.concatenate([w[n, b, a] for a in range(3) for b in range(3)], axis=0)

    for n in range(blocks):
        clear_off_map(pads.at[n], HALO, PAD, PAD)

    def swap(k, start):
        part = pl.ds(start, half)
        return pltpu.make_async_remote_copy(
            src_ref=mirror.at[0, part], dst_ref=mirror.at[1, part],
            send_sem=mirror_sem.at[0, k], recv_sem=mirror_sem.at[1, k],
            device_id={"rows": col, "cols": row}, device_id_type=MESH,
        )

    def mirror_half(k, start):
        part = pl.ds(start, half)
        mirror[0, part] = block_out_of(0, 0, straight(far, 0), start)

        @pl.when(row != col)
        def _():
            swap(k, start).start()

        @pl.when(row == col)
        def _():
            mirror[1, part] = mirror[0, part]

    def columns_half(n, k, end, turn):
        part = slice(end * half, (end + 1) * half)

        @pl.when(row != col)
        def _():
            swap(k, end * half).wait_recv()

        send_columns(n, end, average(turn[part], mirror[1, part]))

    def average_half(n, k, start):
        value = average(
            block_out_of(n, 0, straight(far, n), start),
            block_out_of(n, 1, crossed(far, n), start),
        )
        if n == blocks - 1:
            out_ref[pl.ds(start, half)] = value
        else:
            pads[n + 1, pl.ds(HALO + start, half), body] = value

    load.wait()
    pl.semaphore_wait(barrier, friends)
    send_rows(0)
    state = pads[0, inner, body]
    turn = flip(state)
    send_columns(0, 0, turn)
    send_columns(0, 1, turn)
    send_corners(0, state)
    load_near.wait()
    load_far.wait()

    for n in range(blocks):
        if n == 0:
            halves_of(n, straight(near, n), mirror_half)
            block_out = mirror[0]
            turn = flip(block_out)
            for k in range(2):
                for end in range(2):
                    pl.when(lax.rem(col, 2) == (1 - k if end == 0 else k))(
                        functools.partial(columns_half, n + 1, k, end, turn)
                    )
            state = average(block_out, flip(mirror[1]))
            pads[n + 1, inner, body] = state
            send_rows(n + 1)
            send_corners(n + 1, state)
        else:
            halves_of(
                n, jnp.concatenate([straight(near, n), crossed(near, n)], axis=1),
                functools.partial(average_half, n),
            )
            if n < blocks - 1:
                state = pads[n + 1, inner, body]
                turn = flip(state)
                send_columns(n + 1, 0, turn)
                send_columns(n + 1, 1, turn)
                send_rows(n + 1)
                send_corners(n + 1, state)

    @pl.when(row != col)
    def _():
        for k in range(2):
            swap(k, jnp.where(lax.rem(row, 2) == 1 - k, 0, half)).wait_send()

    for n in range(blocks):
        for at, step in enumerate(SIDES):
            @pl.when(there(step))
            def _():
                rim_copy(n, at).wait_send()


def by_tiles(contact_map, w_near, w_far):
    blocks, channels = w_near.shape[0], w_near.shape[-1]
    side, count = contact_map.shape[0], lax.axis_size("rows")
    kind = contact_map.dtype
    return pl.pallas_call(
        functools.partial(tile_kernel, count, side),
        out_shape=jax.ShapeDtypeStruct(contact_map.shape, kind),
        in_specs=[pl.BlockSpec(memory_space=pltpu.HBM)] * 3,
        out_specs=pl.BlockSpec(memory_space=pltpu.VMEM),
        scratch_shapes=[
            pltpu.VMEM((blocks, side + 2 * HALO, side + 2 * PAD, channels), kind),
            pltpu.VMEM((blocks, 2, HALO, side, channels), kind),
            pltpu.VMEM((blocks, 2, HALO, side, channels), kind),
            pltpu.VMEM((blocks, 2, len(SIDES), HALO * PACK, channels), kind),
            pltpu.VMEM((2, side, side, channels), kind),
            pltpu.VMEM((side + 2 * FAR, side + PAD, 2 * channels), kind),
            pltpu.VMEM(w_near.shape, kind),
            pltpu.VMEM(w_far.shape, kind),
            pltpu.SemaphoreType.DMA((3,)),
            pltpu.SemaphoreType.DMA((blocks, len(SIDES))),
            pltpu.SemaphoreType.DMA((blocks, len(SIDES))),
            pltpu.SemaphoreType.DMA((2, 2)),
        ],
        compiler_params=pltpu.CompilerParams(
            collective_id=0, has_side_effects=True, vmem_limit_bytes=431 * 2**17
        ),
    )(contact_map, w_near, w_far)


def on_device(contact_map, w_near, w_far):
    side = contact_map.shape[0]
    square = side == contact_map.shape[1] and side % PAD == 0
    if square and lax.axis_size("rows") == lax.axis_size("cols") and w_near.shape[0] > 1:
        return by_tiles(contact_map, w_near, w_far)
    return by_rows(contact_map, w_near, w_far)


def solution(mesh):
    in_specs = (P(("groups", "rows"), "cols", None), P(), P())
    out_specs = P(("groups", "rows"), "cols", None)
    return jax.shard_map(
        on_device, mesh=mesh, in_specs=in_specs, out_specs=out_specs, check_vma=False
    )
```

```python
import functools

import jax
import jax.numpy as jnp
from jax import lax
from jax.experimental import pallas as pl
from jax.experimental.pallas import tpu as pltpu
from jax.sharding import PartitionSpec as P

MESH = pl.DeviceIdType.MESH
NEAR, FAR = 2, 4
HALO = NEAR + FAR
PAD, PACK = 16, 8
SIDES = [(-1, 0), (1, 0), (0, -1), (0, 1), (-1, -1), (-1, 1), (1, -1), (1, 1)]


def extended(cells, sides, width):
    for axis, dim in sides:
        count = lax.axis_size(axis)
        ends = count - 1
        head = lax.slice_in_dim(cells, 0, width, axis=dim)
        tail = lax.slice_in_dim(cells, cells.shape[dim] - width, cells.shape[dim], axis=dim)
        cells = jnp.concatenate(
            [
                lax.ppermute(tail, axis, [(i, (i + 1) % count) for i in range(ends)]),
                cells,
                lax.ppermute(head, axis, [((i + 1) % count, i) for i in range(ends)]),
            ],
            axis=dim,
        )
    return cells


def valid_conv(padded, kernel, spread):
    out = lax.conv_general_dilated(
        padded[None],
        kernel,
        (1, 1),
        "VALID",
        rhs_dilation=(spread, spread),
        dimension_numbers=("NHWC", "HWIO", "NHWC"),
        preferred_element_type=jnp.float32,
    )
    return out[0]


def average(block_out, flipped):
    return ((block_out.astype(jnp.float32) + flipped.astype(jnp.float32)) * 0.5).astype(
        jnp.bfloat16
    )


def by_rows(contact_map, w_near, w_far):
    blocks = w_near.shape[0]
    state = lax.all_to_all(contact_map, "cols", split_axis=0, concat_axis=1, tiled=True)
    for block in range(blocks):
        padded = extended(state, ((("rows", "cols"), 0),), NEAR)
        padded = jnp.pad(padded, ((0, 0), (NEAR, NEAR), (0, 0)))
        hidden = jax.nn.relu(valid_conv(padded, w_near[block], NEAR)).astype(jnp.bfloat16)
        padded = extended(hidden, ((("rows", "cols"), 0),), FAR)
        padded = jnp.pad(padded, ((0, 0), (FAR, FAR), (0, 0)))
        block_out = (state.astype(jnp.float32) + valid_conv(padded, w_far[block], FAR)).astype(
            jnp.bfloat16
        )
        mirrored = lax.all_to_all(
            block_out, ("rows", "cols"), split_axis=1, concat_axis=0, tiled=True
        )
        state = average(block_out, jnp.swapaxes(mirrored, 0, 1))
    return lax.all_to_all(state, "cols", split_axis=1, concat_axis=0, tiled=True)


def flip(cells):
    return jnp.transpose(cells, (1, 0, 2))


def tile_kernel(
    count, side, x_ref, near_ref, far_ref, out_ref,
    pads, turned, strips, corners, mirror, hidden, near, far,
    load_sem, send_sem, recv_sem, mirror_sem,
):
    blocks, channels = near_ref.shape[0], near_ref.shape[-1]
    row, col = lax.axis_index("rows"), lax.axis_index("cols")
    last = count - 1
    inner = slice(HALO, HALO + side)
    body = slice(PAD, PAD + side)
    reach = side + 2 * FAR
    span = side + PAD
    half = side // 2

    load = pltpu.make_async_copy(x_ref, pads.at[0, inner, body], load_sem.at[0])
    load.start()

    def there(step):
        di, dj = step
        ok = []
        if di:
            ok.append(row > 0 if di < 0 else row < last)
        if dj:
            ok.append(col > 0 if dj < 0 else col < last)
        return ok[0] if len(ok) == 1 else jnp.logical_and(*ok)

    barrier = pltpu.get_barrier_semaphore()
    friends = (row != col).astype(jnp.int32)

    @pl.when(row != col)
    def _():
        pl.semaphore_signal(
            barrier, inc=1, device_id={"rows": col, "cols": row}, device_id_type=MESH
        )

    for step in SIDES:
        yes = there(step)
        friends += yes.astype(jnp.int32)

        @pl.when(yes)
        def _():
            pl.semaphore_signal(
                barrier, inc=1, device_id={"rows": row + step[0], "cols": col + step[1]},
                device_id_type=MESH,
            )

    load_near = pltpu.make_async_copy(near_ref, near, load_sem.at[1])
    load_far = pltpu.make_async_copy(far_ref, far, load_sem.at[2])
    load_near.start()
    load_far.start()

    def clear(ref):
        ref[...] = jnp.zeros(ref.shape, ref.dtype)

    def clear_off_map(ref, height, left, width):
        for at_edge, part in (
            (row == 0, (slice(0, height), slice(None))),
            (row == last, (slice(height + side, height * 2 + side), slice(None))),
            (col == 0, (slice(None), slice(left - width, left))),
            (col == last, (slice(None), slice(left + side, left + side + width))),
        ):
            pl.when(at_edge)(functools.partial(clear, ref.at[part]))

    def rim_copy(n, at):
        di, dj = SIDES[at]
        if di and dj:
            source, target = corners.at[n, 0, at], corners.at[n, 1, at]
        elif di:
            rows = slice(HALO, 2 * HALO) if di < 0 else slice(side, side + HALO)
            to = slice(HALO + side, 2 * HALO + side) if di < 0 else slice(0, HALO)
            source, target = pads.at[n, rows, body], pads.at[n, to, body]
        else:
            source = turned.at[n, 0 if dj < 0 else 1]
            target = strips.at[n, 1 if dj < 0 else 0]
        return pltpu.make_async_remote_copy(
            src_ref=source, dst_ref=target,
            send_sem=send_sem.at[n, at], recv_sem=recv_sem.at[n, at],
            device_id={"rows": row + di, "cols": col + dj}, device_id_type=MESH,
        )

    def rim_start(n, ats):
        for at in ats:
            @pl.when(there(SIDES[at]))
            def _():
                rim_copy(n, at).start()

    def pack_columns(n, end, turn):
        turned[n, end] = turn[:HALO] if end == 0 else turn[turn.shape[0] - HALO:]

    def pack_corners(n, cells):
        for at in range(4, 8):
            di, dj = SIDES[at]
            rows = slice(0, HALO) if di < 0 else slice(side - HALO, side)
            bins = slice(0, PACK) if dj < 0 else slice(side - PACK, side)
            corners[n, 0, at] = cells[rows, bins].reshape(HALO * PACK, channels)

    def rim_sent(n):
        for at, step in enumerate(SIDES):
            @pl.when(there(step))
            def _():
                rim_copy(n, at).wait_send()

    def rim_wait(n, which):
        for at, (di, dj) in enumerate(SIDES):
            if di != which:
                continue

            @pl.when(there((-di, -dj)))
            def _():
                rim_copy(n, at).wait_recv()
                if not di:
                    bins = slice(PAD - HALO, PAD) if dj > 0 else slice(
                        PAD + side, PAD + side + HALO)
                    pads[n, inner, bins] = flip(strips[n, 0 if dj > 0 else 1])
                elif dj:
                    rows = slice(0, HALO) if di > 0 else slice(HALO + side, 2 * HALO + side)
                    bins = slice(PAD - PACK, PAD) if dj > 0 else slice(
                        PAD + side, PAD + side + PACK)
                    pads[n, rows, bins] = corners[n, 1, at].reshape(HALO, PACK, channels)

    def hidden_rows(n, weights, start, size):
        first, wide = PAD - HALO, weights.shape[1]
        shifted = [
            pads[n, pl.ds(start, size + 2 * NEAR), first + NEAR * b:first + NEAR * b + span]
            for b in range(3)
        ]
        taps = [
            shifted[b][NEAR * a:NEAR * a + size].reshape(size * span, channels)
            for a in range(3) for b in range(3)
        ]
        total = jnp.dot(
            jnp.concatenate(taps, axis=1), weights, preferred_element_type=jnp.float32
        )
        hidden[pl.ds(start, size), :, :wide] = (
            jnp.maximum(total, 0.0).astype(hidden.dtype).reshape(size, span, wide)
        )

    def block_out_of(n, lane, weights, start):
        lanes = slice(lane * channels, (lane + 1) * channels)
        shifted = [
            hidden[pl.ds(start, half + 2 * FAR), FAR * b:FAR * b + side, lanes]
            for b in range(3)
        ]
        taps = [
            shifted[b][FAR * a:FAR * a + half].reshape(half * side, channels)
            for a in range(3) for b in range(3)
        ]
        total = jnp.dot(
            jnp.concatenate(taps, axis=1), weights, preferred_element_type=jnp.float32
        ).reshape(half, side, channels)
        own = pads[n, pl.ds(HALO + start, half), body]
        return (own.astype(jnp.float32) + total).astype(jnp.bfloat16)

    def halves_of(n, weights, half_done, between):
        rim_wait(n, 0)
        hidden_rows(n, weights, HALO, side - 2 * NEAR)
        for k in range(2):
            above = lax.rem(row, 2) == 1 - k
            pl.when(above)(functools.partial(rim_wait, n, 1))
            pl.when(jnp.logical_not(above))(functools.partial(rim_wait, n, -1))
            hidden_rows(n, weights, jnp.where(above, 0, reach - HALO), HALO)
            clear_off_map(hidden, FAR, FAR, FAR)
            half_done(k, jnp.where(above, 0, half))
            if k == 0:
                between()

    def straight(w, n):
        return w[n].reshape(9 * channels, channels)

    def crossed(w, n):
        return jnp.concatenate([w[n, b, a] for a in range(3) for b in range(3)], axis=0)

    for n in range(blocks):
        clear_off_map(pads.at[n], HALO, PAD, PAD)

    def swap(k, start):
        part = pl.ds(start, half)
        return pltpu.make_async_remote_copy(
            src_ref=mirror.at[0, part], dst_ref=mirror.at[1, part],
            send_sem=mirror_sem.at[0, k], recv_sem=mirror_sem.at[1, k],
            device_id={"rows": col, "cols": row}, device_id_type=MESH,
        )

    def mirror_half(k, start):
        part = pl.ds(start, half)
        mirror[0, part] = block_out_of(0, 0, straight(far, 0), start)

        @pl.when(row != col)
        def _():
            swap(k, start).start()

        @pl.when(row == col)
        def _():
            mirror[1, part] = mirror[0, part]

    def columns_half(n, k, end, turn):
        part = slice(end * half, (end + 1) * half)

        @pl.when(row != col)
        def _():
            swap(k, end * half).wait_recv()

        pack_columns(n, end, average(turn[part], mirror[1, part]))
        rim_start(n, (2 + end,))

    def average_half(n, k, start):
        value = average(
            block_out_of(n, 0, straight(far, n), start),
            block_out_of(n, 1, crossed(far, n), start),
        )
        if n == blocks - 1:
            out_ref[pl.ds(start, half)] = value
        else:
            pads[n + 1, pl.ds(HALO + start, half), body] = value

    def mirror_sent():
        @pl.when(row != col)
        def _():
            for k in range(2):
                swap(k, jnp.where(lax.rem(row, 2) == 1 - k, 0, half)).wait_send()

    load.wait()
    state = pads[0, inner, body]
    turn = flip(state)
    pack_columns(0, 0, turn)
    pack_columns(0, 1, turn)
    pack_corners(0, state)
    pl.semaphore_wait(barrier, friends)
    rim_start(0, (2, 3, 0, 1, 4, 5, 6, 7))
    load_near.wait()
    load_far.wait()

    for n in range(blocks):
        if n == 0:
            halves_of(n, straight(near, n), mirror_half, lambda: None)
            block_out = mirror[0]
            turn = flip(block_out)
            rim_sent(n)
            for k in range(2):
                for end in range(2):
                    pl.when(lax.rem(col, 2) == (1 - k if end == 0 else k))(
                        functools.partial(columns_half, n + 1, k, end, turn)
                    )
            state = average(block_out, flip(mirror[1]))
            pads[n + 1, inner, body] = state
            rim_start(n + 1, (0, 1))
            pack_corners(n + 1, state)
            rim_start(n + 1, (4, 5, 6, 7))
            mirror_sent()
        else:
            halves_of(
                n, jnp.concatenate([straight(near, n), crossed(near, n)], axis=1),
                functools.partial(average_half, n), functools.partial(rim_sent, n),
            )
            if n < blocks - 1:
                state = pads[n + 1, inner, body]
                turn = flip(state)
                pack_columns(n + 1, 0, turn)
                pack_columns(n + 1, 1, turn)
                pack_corners(n + 1, state)
                rim_start(n + 1, (2, 3, 0, 1, 4, 5, 6, 7))


def by_tiles(contact_map, w_near, w_far):
    blocks, channels = w_near.shape[0], w_near.shape[-1]
    side, count = contact_map.shape[0], lax.axis_size("rows")
    kind = contact_map.dtype
    return pl.pallas_call(
        functools.partial(tile_kernel, count, side),
        out_shape=jax.ShapeDtypeStruct(contact_map.shape, kind),
        in_specs=[pl.BlockSpec(memory_space=pltpu.HBM)] * 3,
        out_specs=pl.BlockSpec(memory_space=pltpu.VMEM),
        scratch_shapes=[
            pltpu.VMEM((blocks, side + 2 * HALO, side + 2 * PAD, channels), kind),
            pltpu.VMEM((blocks, 2, HALO, side, channels), kind),
            pltpu.VMEM((blocks, 2, HALO, side, channels), kind),
            pltpu.VMEM((blocks, 2, len(SIDES), HALO * PACK, channels), kind),
            pltpu.VMEM((2, side, side, channels), kind),
            pltpu.VMEM((side + 2 * FAR, side + PAD, 2 * channels), kind),
            pltpu.VMEM(w_near.shape, kind),
            pltpu.VMEM(w_far.shape, kind),
            pltpu.SemaphoreType.DMA((3,)),
            pltpu.SemaphoreType.DMA((blocks, len(SIDES))),
            pltpu.SemaphoreType.DMA((blocks, len(SIDES))),
            pltpu.SemaphoreType.DMA((2, 2)),
        ],
        compiler_params=pltpu.CompilerParams(
            collective_id=0, has_side_effects=True, vmem_limit_bytes=431 * 2**17
        ),
    )(contact_map, w_near, w_far)


def on_device(contact_map, w_near, w_far):
    side = contact_map.shape[0]
    square = side == contact_map.shape[1] and side % PAD == 0
    if square and lax.axis_size("rows") == lax.axis_size("cols") and w_near.shape[0] > 1:
        return by_tiles(contact_map, w_near, w_far)
    return by_rows(contact_map, w_near, w_far)


def solution(mesh):
    in_specs = (P(("groups", "rows"), "cols", None), P(), P())
    out_specs = P(("groups", "rows"), "cols", None)
    return jax.shard_map(
        on_device, mesh=mesh, in_specs=in_specs, out_specs=out_specs, check_vma=False
    )
```

```python
import functools

import jax
import jax.numpy as jnp
from jax import lax
from jax.experimental import pallas as pl
from jax.experimental.pallas import tpu as pltpu
from jax.sharding import PartitionSpec as P

MESH = pl.DeviceIdType.MESH
NEAR, FAR = 2, 4
HALO = NEAR + FAR
PAD, PACK = 16, 8
SIDES = [(-1, 0), (1, 0), (0, -1), (0, 1), (-1, -1), (-1, 1), (1, -1), (1, 1)]


def extended(cells, sides, width):
    for axis, dim in sides:
        count = lax.axis_size(axis)
        ends = count - 1
        head = lax.slice_in_dim(cells, 0, width, axis=dim)
        tail = lax.slice_in_dim(cells, cells.shape[dim] - width, cells.shape[dim], axis=dim)
        cells = jnp.concatenate(
            [
                lax.ppermute(tail, axis, [(i, (i + 1) % count) for i in range(ends)]),
                cells,
                lax.ppermute(head, axis, [((i + 1) % count, i) for i in range(ends)]),
            ],
            axis=dim,
        )
    return cells


def valid_conv(padded, kernel, spread):
    out = lax.conv_general_dilated(
        padded[None],
        kernel,
        (1, 1),
        "VALID",
        rhs_dilation=(spread, spread),
        dimension_numbers=("NHWC", "HWIO", "NHWC"),
        preferred_element_type=jnp.float32,
    )
    return out[0]


def average(block_out, flipped):
    return ((block_out.astype(jnp.float32) + flipped.astype(jnp.float32)) * 0.5).astype(
        jnp.bfloat16
    )


def by_rows(contact_map, w_near, w_far):
    blocks = w_near.shape[0]
    state = lax.all_to_all(contact_map, "cols", split_axis=0, concat_axis=1, tiled=True)
    for block in range(blocks):
        padded = extended(state, ((("rows", "cols"), 0),), NEAR)
        padded = jnp.pad(padded, ((0, 0), (NEAR, NEAR), (0, 0)))
        hidden = jax.nn.relu(valid_conv(padded, w_near[block], NEAR)).astype(jnp.bfloat16)
        padded = extended(hidden, ((("rows", "cols"), 0),), FAR)
        padded = jnp.pad(padded, ((0, 0), (FAR, FAR), (0, 0)))
        block_out = (state.astype(jnp.float32) + valid_conv(padded, w_far[block], FAR)).astype(
            jnp.bfloat16
        )
        mirrored = lax.all_to_all(
            block_out, ("rows", "cols"), split_axis=1, concat_axis=0, tiled=True
        )
        state = average(block_out, jnp.swapaxes(mirrored, 0, 1))
    return lax.all_to_all(state, "cols", split_axis=1, concat_axis=0, tiled=True)


def flip(cells):
    return jnp.transpose(cells, (1, 0, 2))


def tile_kernel(
    count, side, x_ref, near_ref, far_ref, out_ref,
    pads, turned, strips, corners, mirror, hidden, near, far,
    load_sem, send_sem, recv_sem, mirror_sem,
):
    blocks, channels = near_ref.shape[0], near_ref.shape[-1]
    row, col = lax.axis_index("rows"), lax.axis_index("cols")
    last = count - 1
    inner = slice(HALO, HALO + side)
    body = slice(PAD, PAD + side)
    reach = side + 2 * FAR
    span = side + PAD
    half = side // 2

    load = pltpu.make_async_copy(x_ref, pads.at[0, inner, body], load_sem.at[0])
    load.start()

    def there(step):
        di, dj = step
        ok = []
        if di:
            ok.append(row > 0 if di < 0 else row < last)
        if dj:
            ok.append(col > 0 if dj < 0 else col < last)
        return ok[0] if len(ok) == 1 else jnp.logical_and(*ok)

    barrier = pltpu.get_barrier_semaphore()
    friends = (row != col).astype(jnp.int32)

    @pl.when(row != col)
    def _():
        pl.semaphore_signal(
            barrier, inc=1, device_id={"rows": col, "cols": row}, device_id_type=MESH
        )

    for step in SIDES:
        yes = there(step)
        friends += yes.astype(jnp.int32)

        @pl.when(yes)
        def _():
            pl.semaphore_signal(
                barrier, inc=1, device_id={"rows": row + step[0], "cols": col + step[1]},
                device_id_type=MESH,
            )

    load_near = pltpu.make_async_copy(near_ref, near, load_sem.at[1])
    load_far = pltpu.make_async_copy(far_ref, far, load_sem.at[2])
    load_near.start()
    load_far.start()

    def clear(ref):
        ref[...] = jnp.zeros(ref.shape, ref.dtype)

    def clear_off_map(ref, height, left, width):
        for at_edge, part in (
            (row == 0, (slice(0, height), slice(None))),
            (row == last, (slice(height + side, height * 2 + side), slice(None))),
            (col == 0, (slice(None), slice(left - width, left))),
            (col == last, (slice(None), slice(left + side, left + side + width))),
        ):
            pl.when(at_edge)(functools.partial(clear, ref.at[part]))

    def rim_copy(n, at):
        di, dj = SIDES[at]
        if di and dj:
            source, target = corners.at[n, 0, at], corners.at[n, 1, at]
        elif di:
            rows = slice(HALO, 2 * HALO) if di < 0 else slice(side, side + HALO)
            to = slice(HALO + side, 2 * HALO + side) if di < 0 else slice(0, HALO)
            source, target = pads.at[n, rows, body], pads.at[n, to, body]
        else:
            source = turned.at[n, 0 if dj < 0 else 1]
            target = strips.at[n, 1 if dj < 0 else 0]
        return pltpu.make_async_remote_copy(
            src_ref=source, dst_ref=target,
            send_sem=send_sem.at[n, at], recv_sem=recv_sem.at[n, at],
            device_id={"rows": row + di, "cols": col + dj}, device_id_type=MESH,
        )

    def rim_start(n, ats):
        for at in ats:
            @pl.when(there(SIDES[at]))
            def _():
                rim_copy(n, at).start()

    def pack_columns(n, end, turn):
        turned[n, end] = turn[:HALO] if end == 0 else turn[turn.shape[0] - HALO:]

    def pack_corners(n, cells):
        for at in range(4, 8):
            di, dj = SIDES[at]
            rows = slice(0, HALO) if di < 0 else slice(side - HALO, side)
            bins = slice(0, PACK) if dj < 0 else slice(side - PACK, side)
            corners[n, 0, at] = cells[rows, bins].reshape(HALO * PACK, channels)

    def rim_sent(n):
        for at, step in enumerate(SIDES):
            @pl.when(there(step))
            def _():
                rim_copy(n, at).wait_send()

    def rim_wait(n, which):
        for at, (di, dj) in enumerate(SIDES):
            if di != which:
                continue

            @pl.when(there((-di, -dj)))
            def _():
                rim_copy(n, at).wait_recv()
                if not di:
                    bins = slice(PAD - HALO, PAD) if dj > 0 else slice(
                        PAD + side, PAD + side + HALO)
                    pads[n, inner, bins] = flip(strips[n, 0 if dj > 0 else 1])
                elif dj:
                    rows = slice(0, HALO) if di > 0 else slice(HALO + side, 2 * HALO + side)
                    bins = slice(PAD - PACK, PAD) if dj > 0 else slice(
                        PAD + side, PAD + side + PACK)
                    pads[n, rows, bins] = corners[n, 1, at].reshape(HALO, PACK, channels)

    def hidden_rows(n, weights, start, size):
        first, wide = PAD - HALO, weights.shape[1]
        shifted = [
            pads[n, pl.ds(start, size + 2 * NEAR), first + NEAR * b:first + NEAR * b + span]
            for b in range(3)
        ]
        taps = [
            shifted[b][NEAR * a:NEAR * a + size].reshape(size * span, channels)
            for a in range(3) for b in range(3)
        ]
        total = jnp.dot(
            jnp.concatenate(taps, axis=1), weights, preferred_element_type=jnp.float32
        )
        hidden[pl.ds(start, size), :, :wide] = (
            jnp.maximum(total, 0.0).astype(hidden.dtype).reshape(size, span, wide)
        )

    def block_out_of(n, lane, weights, start):
        lanes = slice(lane * channels, (lane + 1) * channels)
        shifted = [
            hidden[pl.ds(start, half + 2 * FAR), FAR * b:FAR * b + side, lanes]
            for b in range(3)
        ]
        taps = [
            shifted[b][FAR * a:FAR * a + half].reshape(half * side, channels)
            for a in range(3) for b in range(3)
        ]
        total = jnp.dot(
            jnp.concatenate(taps, axis=1), weights, preferred_element_type=jnp.float32
        ).reshape(half, side, channels)
        own = pads[n, pl.ds(HALO + start, half), body]
        return (own.astype(jnp.float32) + total).astype(jnp.bfloat16)

    def halves_of(n, weights, half_done):
        rim_wait(n, 0)
        hidden_rows(n, weights, HALO, side - 2 * NEAR)

        @pl.loop(0, 2)
        def _(k):
            above = lax.rem(row, 2) == 1 - k
            pl.when(above)(functools.partial(rim_wait, n, 1))
            pl.when(jnp.logical_not(above))(functools.partial(rim_wait, n, -1))
            hidden_rows(n, weights, jnp.where(above, 0, reach - HALO), HALO)
            clear_off_map(hidden, FAR, FAR, FAR)
            half_done(k, jnp.where(above, 0, half))

    def straight(w, n):
        return w[n].reshape(9 * channels, channels)

    def crossed(w, n):
        return jnp.concatenate([w[n, b, a] for a in range(3) for b in range(3)], axis=0)

    for n in range(blocks):
        clear_off_map(pads.at[n], HALO, PAD, PAD)

    def swap(k, start):
        part = pl.ds(start, half)
        return pltpu.make_async_remote_copy(
            src_ref=mirror.at[0, part], dst_ref=mirror.at[1, part],
            send_sem=mirror_sem.at[0, k], recv_sem=mirror_sem.at[1, k],
            device_id={"rows": col, "cols": row}, device_id_type=MESH,
        )

    def mirror_half(k, start):
        part = pl.ds(start, half)
        mirror[0, part] = block_out_of(0, 0, straight(far, 0), start)

        @pl.when(row != col)
        def _():
            swap(k, start).start()

        @pl.when(row == col)
        def _():
            mirror[1, part] = mirror[0, part]

    def columns_half(n, k, end, turn):
        part = slice(end * half, (end + 1) * half)

        @pl.when(row != col)
        def _():
            swap(k, end * half).wait_recv()

        pack_columns(n, end, average(turn[part], mirror[1, part]))
        rim_start(n, (2 + end,))

    def average_half(n, k, start):
        value = average(
            block_out_of(n, 0, straight(far, n), start),
            block_out_of(n, 1, crossed(far, n), start),
        )
        if n == blocks - 1:
            out_ref[pl.ds(start, half)] = value
        else:
            pads[n + 1, pl.ds(HALO + start, half), body] = value

    def mirror_sent():
        @pl.when(row != col)
        def _():
            for k in range(2):
                swap(k, jnp.where(lax.rem(row, 2) == 1 - k, 0, half)).wait_send()

    load.wait()
    state = pads[0, inner, body]
    turn = flip(state)
    pack_columns(0, 0, turn)
    pack_columns(0, 1, turn)
    pack_corners(0, state)
    pl.semaphore_wait(barrier, friends)
    rim_start(0, (2, 3, 0, 1, 4, 5, 6, 7))
    load_near.wait()
    load_far.wait()

    for n in range(blocks):
        if n == 0:
            halves_of(n, straight(near, n), mirror_half)
            block_out = mirror[0]
            turn = flip(block_out)
            rim_sent(n)
            for k in range(2):
                for end in range(2):
                    pl.when(lax.rem(col, 2) == (1 - k if end == 0 else k))(
                        functools.partial(columns_half, n + 1, k, end, turn)
                    )
            state = average(block_out, flip(mirror[1]))
            pads[n + 1, inner, body] = state
            rim_start(n + 1, (0, 1))
            pack_corners(n + 1, state)
            rim_start(n + 1, (4, 5, 6, 7))
            mirror_sent()
        else:
            halves_of(
                n, jnp.concatenate([straight(near, n), crossed(near, n)], axis=1),
                functools.partial(average_half, n),
            )
            rim_sent(n)
            if n < blocks - 1:
                state = pads[n + 1, inner, body]
                turn = flip(state)
                pack_columns(n + 1, 0, turn)
                pack_columns(n + 1, 1, turn)
                pack_corners(n + 1, state)
                rim_start(n + 1, (2, 3, 0, 1, 4, 5, 6, 7))


def by_tiles(contact_map, w_near, w_far):
    blocks, channels = w_near.shape[0], w_near.shape[-1]
    side, count = contact_map.shape[0], lax.axis_size("rows")
    kind = contact_map.dtype
    return pl.pallas_call(
        functools.partial(tile_kernel, count, side),
        out_shape=jax.ShapeDtypeStruct(contact_map.shape, kind),
        in_specs=[pl.BlockSpec(memory_space=pltpu.HBM)] * 3,
        out_specs=pl.BlockSpec(memory_space=pltpu.VMEM),
        scratch_shapes=[
            pltpu.VMEM((blocks, side + 2 * HALO, side + 2 * PAD, channels), kind),
            pltpu.VMEM((blocks, 2, HALO, side, channels), kind),
            pltpu.VMEM((blocks, 2, HALO, side, channels), kind),
            pltpu.VMEM((blocks, 2, len(SIDES), HALO * PACK, channels), kind),
            pltpu.VMEM((2, side, side, channels), kind),
            pltpu.VMEM((side + 2 * FAR, side + PAD, 2 * channels), kind),
            pltpu.VMEM(w_near.shape, kind),
            pltpu.VMEM(w_far.shape, kind),
            pltpu.SemaphoreType.DMA((3,)),
            pltpu.SemaphoreType.DMA((blocks, len(SIDES))),
            pltpu.SemaphoreType.DMA((blocks, len(SIDES))),
            pltpu.SemaphoreType.DMA((2, 2)),
        ],
        compiler_params=pltpu.CompilerParams(
            collective_id=0, has_side_effects=True, vmem_limit_bytes=431 * 2**17
        ),
    )(contact_map, w_near, w_far)


def on_device(contact_map, w_near, w_far):
    side = contact_map.shape[0]
    square = side == contact_map.shape[1] and side % PAD == 0
    if square and lax.axis_size("rows") == lax.axis_size("cols") and w_near.shape[0] > 1:
        return by_tiles(contact_map, w_near, w_far)
    return by_rows(contact_map, w_near, w_far)


def solution(mesh):
    in_specs = (P(("groups", "rows"), "cols", None), P(), P())
    out_specs = P(("groups", "rows"), "cols", None)
    return jax.shard_map(
        on_device, mesh=mesh, in_specs=in_specs, out_specs=out_specs, check_vma=False
    )
```

```python
import functools

import jax
import jax.numpy as jnp
from jax import lax
from jax.experimental import pallas as pl
from jax.experimental.pallas import tpu as pltpu
from jax.sharding import PartitionSpec as P

MESH = pl.DeviceIdType.MESH
NEAR, FAR = 2, 4
HALO = NEAR + FAR
PAD, PACK = 16, 8
SIDES = [(-1, 0), (1, 0), (0, -1), (0, 1), (-1, -1), (-1, 1), (1, -1), (1, 1)]


def extended(cells, sides, width):
    for axis, dim in sides:
        count = lax.axis_size(axis)
        ends = count - 1
        head = lax.slice_in_dim(cells, 0, width, axis=dim)
        tail = lax.slice_in_dim(cells, cells.shape[dim] - width, cells.shape[dim], axis=dim)
        cells = jnp.concatenate(
            [
                lax.ppermute(tail, axis, [(i, (i + 1) % count) for i in range(ends)]),
                cells,
                lax.ppermute(head, axis, [((i + 1) % count, i) for i in range(ends)]),
            ],
            axis=dim,
        )
    return cells


def valid_conv(padded, kernel, spread):
    out = lax.conv_general_dilated(
        padded[None],
        kernel,
        (1, 1),
        "VALID",
        rhs_dilation=(spread, spread),
        dimension_numbers=("NHWC", "HWIO", "NHWC"),
        preferred_element_type=jnp.float32,
    )
    return out[0]


def average(block_out, flipped):
    return ((block_out.astype(jnp.float32) + flipped.astype(jnp.float32)) * 0.5).astype(
        jnp.bfloat16
    )


def by_rows(contact_map, w_near, w_far):
    blocks = w_near.shape[0]
    state = lax.all_to_all(contact_map, "cols", split_axis=0, concat_axis=1, tiled=True)
    for block in range(blocks):
        padded = extended(state, ((("rows", "cols"), 0),), NEAR)
        padded = jnp.pad(padded, ((0, 0), (NEAR, NEAR), (0, 0)))
        hidden = jax.nn.relu(valid_conv(padded, w_near[block], NEAR)).astype(jnp.bfloat16)
        padded = extended(hidden, ((("rows", "cols"), 0),), FAR)
        padded = jnp.pad(padded, ((0, 0), (FAR, FAR), (0, 0)))
        block_out = (state.astype(jnp.float32) + valid_conv(padded, w_far[block], FAR)).astype(
            jnp.bfloat16
        )
        mirrored = lax.all_to_all(
            block_out, ("rows", "cols"), split_axis=1, concat_axis=0, tiled=True
        )
        state = average(block_out, jnp.swapaxes(mirrored, 0, 1))
    return lax.all_to_all(state, "cols", split_axis=1, concat_axis=0, tiled=True)


def flip(cells):
    return jnp.transpose(cells, (1, 0, 2))


def tile_kernel(
    count, side, x_ref, near_ref, far_ref, out_ref,
    pads, turned, strips, corners, mirror, hidden, near, far,
    load_sem, send_sem, recv_sem, mirror_sem,
):
    blocks, channels = near_ref.shape[0], near_ref.shape[-1]
    row, col = lax.axis_index("rows"), lax.axis_index("cols")
    last = count - 1
    inner = slice(HALO, HALO + side)
    body = slice(PAD, PAD + side)
    reach = side + 2 * FAR
    span = side + PAD
    half = side // 2

    load = pltpu.make_async_copy(x_ref, pads.at[0, inner, body], load_sem.at[0])
    load.start()

    def there(step):
        di, dj = step
        ok = []
        if di:
            ok.append(row > 0 if di < 0 else row < last)
        if dj:
            ok.append(col > 0 if dj < 0 else col < last)
        return ok[0] if len(ok) == 1 else jnp.logical_and(*ok)

    barrier = pltpu.get_barrier_semaphore()
    friends = (row != col).astype(jnp.int32)

    @pl.when(row != col)
    def _():
        pl.semaphore_signal(
            barrier, inc=1, device_id={"rows": col, "cols": row}, device_id_type=MESH
        )

    for step in SIDES:
        yes = there(step)
        friends += yes.astype(jnp.int32)

        @pl.when(yes)
        def _():
            pl.semaphore_signal(
                barrier, inc=1, device_id={"rows": row + step[0], "cols": col + step[1]},
                device_id_type=MESH,
            )

    load_near = pltpu.make_async_copy(near_ref, near, load_sem.at[1])
    load_far = pltpu.make_async_copy(far_ref, far, load_sem.at[2])
    load_near.start()
    load_far.start()

    def clear(ref):
        ref[...] = jnp.zeros(ref.shape, ref.dtype)

    def clear_off_map(ref, height, left, width):
        for at_edge, part in (
            (row == 0, (slice(0, height), slice(None))),
            (row == last, (slice(height + side, height * 2 + side), slice(None))),
            (col == 0, (slice(None), slice(left - width, left))),
            (col == last, (slice(None), slice(left + side, left + side + width))),
        ):
            pl.when(at_edge)(functools.partial(clear, ref.at[part]))

    def rim_copy(n, at):
        di, dj = SIDES[at]
        if di and dj:
            source, target = corners.at[n, 0, at], corners.at[n, 1, at]
        elif di:
            rows = slice(HALO, 2 * HALO) if di < 0 else slice(side, side + HALO)
            to = slice(HALO + side, 2 * HALO + side) if di < 0 else slice(0, HALO)
            source, target = pads.at[n, rows, body], pads.at[n, to, body]
        else:
            source = turned.at[n, slice(0, HALO) if dj < 0 else slice(side - HALO, side)]
            target = strips.at[n, 1 if dj < 0 else 0]
        return pltpu.make_async_remote_copy(
            src_ref=source, dst_ref=target,
            send_sem=send_sem.at[n, at], recv_sem=recv_sem.at[n, at],
            device_id={"rows": row + di, "cols": col + dj}, device_id_type=MESH,
        )

    def rim_start(n, ats):
        for at in ats:
            @pl.when(there(SIDES[at]))
            def _():
                rim_copy(n, at).start()

    def pack_corners(n, cells):
        for at in range(4, 8):
            di, dj = SIDES[at]
            rows = slice(0, HALO) if di < 0 else slice(side - HALO, side)
            bins = slice(0, PACK) if dj < 0 else slice(side - PACK, side)
            corners[n, 0, at] = cells[rows, bins].reshape(HALO * PACK, channels)

    def rim_sent(n):
        for at, step in enumerate(SIDES):
            @pl.when(there(step))
            def _():
                rim_copy(n, at).wait_send()

    def wait_columns(n):
        for at in (2, 3):
            dj = SIDES[at][1]

            @pl.when(there((0, -dj)))
            def _():
                rim_copy(n, at).wait_recv()
                bins = slice(PAD - HALO, PAD) if dj > 0 else slice(
                    PAD + side, PAD + side + HALO)
                pads[n, inner, bins] = flip(strips[n, 0 if dj > 0 else 1])

    def wait_rows(n, above):
        down = above.astype(jnp.int32)
        rows = pl.ds(jnp.where(above, 0, HALO + side), HALO)

        def landed(ref, at):
            pltpu.make_async_remote_copy(
                src_ref=ref, dst_ref=ref,
                send_sem=send_sem.at[n, at], recv_sem=recv_sem.at[n, at],
                device_id={"rows": row, "cols": col}, device_id_type=MESH,
            ).wait_recv()

        @pl.when(jnp.where(above, row, last - row) > 0)
        def _():
            landed(pads.at[n, rows, body], down)
            for right, dj in enumerate((-1, 1)):
                at = 4 + 2 * down + right

                @pl.when(col < last if dj < 0 else col > 0)
                def _():
                    landed(corners.at[n, 1, at], at)
                    bins = slice(PAD - PACK, PAD) if dj > 0 else slice(
                        PAD + side, PAD + side + PACK)
                    pads[n, rows, bins] = corners[n, 1, at].reshape(HALO, PACK, channels)

    def hidden_rows(n, weights, start, size):
        first, wide = PAD - HALO, weights.shape[1]
        shifted = [
            pads[n, pl.ds(start, size + 2 * NEAR), first + NEAR * b:first + NEAR * b + span]
            for b in range(3)
        ]
        taps = [
            shifted[b][NEAR * a:NEAR * a + size].reshape(size * span, channels)
            for a in range(3) for b in range(3)
        ]
        total = jnp.dot(
            jnp.concatenate(taps, axis=1), weights, preferred_element_type=jnp.float32
        )
        hidden[pl.ds(start, size), :, :wide] = (
            jnp.maximum(total, 0.0).astype(hidden.dtype).reshape(size, span, wide)
        )

    def block_out_of(n, lane, weights, start):
        lanes = slice(lane * channels, (lane + 1) * channels)
        shifted = [
            hidden[pl.ds(start, half + 2 * FAR), FAR * b:FAR * b + side, lanes]
            for b in range(3)
        ]
        taps = [
            shifted[b][FAR * a:FAR * a + half].reshape(half * side, channels)
            for a in range(3) for b in range(3)
        ]
        total = jnp.dot(
            jnp.concatenate(taps, axis=1), weights, preferred_element_type=jnp.float32
        ).reshape(half, side, channels)
        own = pads[n, pl.ds(HALO + start, half), body]
        return (own.astype(jnp.float32) + total).astype(jnp.bfloat16)

    def halves_of(n, weights, half_done):
        wait_columns(n)
        middle = -(-(side - 2 * NEAR) // HALO)

        @pl.loop(0, middle + 2)
        def _(step):
            k = step - middle
            above = lax.rem(row, 2) == 1 - k

            @pl.when(k >= 0)
            def _():
                wait_rows(n, above)

            between = jnp.minimum(HALO * (step + 1), reach - 2 * HALO)
            ends = jnp.where(above, 0, reach - HALO)
            hidden_rows(n, weights(), jnp.where(k < 0, between, ends), HALO)

            @pl.when(k >= 0)
            def _():
                clear_off_map(hidden, FAR, FAR, FAR)
                half_done(k, jnp.where(above, 0, half))

    def straight(w, n):
        return w[n].reshape(9 * channels, channels)

    def crossed(w, n):
        return jnp.concatenate([w[n, b, a] for a in range(3) for b in range(3)], axis=0)

    for n in range(blocks):
        clear_off_map(pads.at[n], HALO, PAD, PAD)

    def swap(k, start):
        part = pl.ds(start, half)
        return pltpu.make_async_remote_copy(
            src_ref=mirror.at[0, part], dst_ref=mirror.at[1, part],
            send_sem=mirror_sem.at[0, k], recv_sem=mirror_sem.at[1, k],
            device_id={"rows": col, "cols": row}, device_id_type=MESH,
        )

    def mirror_half(k, start):
        part = pl.ds(start, half)
        mirror[0, part] = block_out_of(0, 0, straight(far, 0), start)

        @pl.when(row != col)
        def _():
            swap(k, start).start()

        @pl.when(row == col)
        def _():
            mirror[1, part] = mirror[0, part]

    def columns_half(n, k):
        end = jnp.where(lax.rem(col, 2) == 1 - k, 0, 1)
        part = pl.ds(end * half, half)

        @pl.when(row != col)
        def _():
            swap(k, end * half).wait_recv()

        turned[n, part] = average(turned[n, part], mirror[1, part])
        for at in (2, 3):
            pl.when(end == at - 2)(functools.partial(rim_start, n, (at,)))

    def average_half(n, k, start):
        value = average(
            block_out_of(n, 0, straight(far, n), start),
            block_out_of(n, 1, crossed(far, n), start),
        )
        if n == blocks - 1:
            out_ref[pl.ds(start, half)] = value
        else:
            pads[n + 1, pl.ds(HALO + start, half), body] = value

    def mirror_sent():
        @pl.when(row != col)
        def _():
            for k in range(2):
                swap(k, jnp.where(lax.rem(row, 2) == 1 - k, 0, half)).wait_send()

    load.wait()
    state = pads[0, inner, body]
    turned[0] = flip(state)
    pack_corners(0, state)
    pl.semaphore_wait(barrier, friends)
    rim_start(0, (2, 3, 0, 1, 4, 5, 6, 7))
    load_near.wait()
    load_far.wait()

    for n in range(blocks):
        if n == 0:
            halves_of(n, lambda: straight(near, n), mirror_half)
            turned[n + 1] = flip(mirror[0])
            rim_sent(n)
            pl.loop(0, 2)(functools.partial(columns_half, n + 1))
            state = flip(turned[n + 1])
            pads[n + 1, inner, body] = state
            rim_start(n + 1, (0, 1))
            pack_corners(n + 1, state)
            rim_start(n + 1, (4, 5, 6, 7))
            mirror_sent()
        else:
            halves_of(
                n, lambda: jnp.concatenate([straight(near, n), crossed(near, n)], axis=1),
                functools.partial(average_half, n),
            )
            rim_sent(n)
            if n < blocks - 1:
                state = pads[n + 1, inner, body]
                turned[n + 1] = flip(state)
                pack_corners(n + 1, state)
                rim_start(n + 1, (2, 3, 0, 1, 4, 5, 6, 7))


def by_tiles(contact_map, w_near, w_far):
    blocks, channels = w_near.shape[0], w_near.shape[-1]
    side, count = contact_map.shape[0], lax.axis_size("rows")
    kind = contact_map.dtype
    return pl.pallas_call(
        functools.partial(tile_kernel, count, side),
        out_shape=jax.ShapeDtypeStruct(contact_map.shape, kind),
        in_specs=[pl.BlockSpec(memory_space=pltpu.HBM)] * 3,
        out_specs=pl.BlockSpec(memory_space=pltpu.VMEM),
        scratch_shapes=[
            pltpu.VMEM((blocks, side + 2 * HALO, side + 2 * PAD, channels), kind),
            pltpu.VMEM((blocks, side, side, channels), kind),
            pltpu.VMEM((blocks, 2, HALO, side, channels), kind),
            pltpu.VMEM((blocks, 2, len(SIDES), HALO * PACK, channels), kind),
            pltpu.VMEM((2, side, side, channels), kind),
            pltpu.VMEM((side + 2 * FAR, side + PAD, 2 * channels), kind),
            pltpu.VMEM(w_near.shape, kind),
            pltpu.VMEM(w_far.shape, kind),
            pltpu.SemaphoreType.DMA((3,)),
            pltpu.SemaphoreType.DMA((blocks, len(SIDES))),
            pltpu.SemaphoreType.DMA((blocks, len(SIDES))),
            pltpu.SemaphoreType.DMA((2, 2)),
        ],
        compiler_params=pltpu.CompilerParams(
            collective_id=0, has_side_effects=True, vmem_limit_bytes=431 * 2**17
        ),
    )(contact_map, w_near, w_far)


def on_device(contact_map, w_near, w_far):
    side = contact_map.shape[0]
    square = side == contact_map.shape[1] and side % PAD == 0
    if square and lax.axis_size("rows") == lax.axis_size("cols") and w_near.shape[0] > 1:
        return by_tiles(contact_map, w_near, w_far)
    return by_rows(contact_map, w_near, w_far)


def solution(mesh):
    in_specs = (P(("groups", "rows"), "cols", None), P(), P())
    out_specs = P(("groups", "rows"), "cols", None)
    return jax.shard_map(
        on_device, mesh=mesh, in_specs=in_specs, out_specs=out_specs, check_vma=False
    )
```

```python
import functools

import jax
import jax.numpy as jnp
from jax import lax
from jax.experimental import pallas as pl
from jax.experimental.pallas import tpu as pltpu
from jax.sharding import PartitionSpec as P

MESH = pl.DeviceIdType.MESH
NEAR, FAR = 2, 4
HALO = NEAR + FAR
PAD, PACK = 16, 8
SIDES = [(-1, 0), (1, 0), (0, -1), (0, 1), (-1, -1), (-1, 1), (1, -1), (1, 1)]


def extended(cells, sides, width):
    for axis, dim in sides:
        count = lax.axis_size(axis)
        ends = count - 1
        head = lax.slice_in_dim(cells, 0, width, axis=dim)
        tail = lax.slice_in_dim(cells, cells.shape[dim] - width, cells.shape[dim], axis=dim)
        cells = jnp.concatenate(
            [
                lax.ppermute(tail, axis, [(i, (i + 1) % count) for i in range(ends)]),
                cells,
                lax.ppermute(head, axis, [((i + 1) % count, i) for i in range(ends)]),
            ],
            axis=dim,
        )
    return cells


def valid_conv(padded, kernel, spread):
    out = lax.conv_general_dilated(
        padded[None],
        kernel,
        (1, 1),
        "VALID",
        rhs_dilation=(spread, spread),
        dimension_numbers=("NHWC", "HWIO", "NHWC"),
        preferred_element_type=jnp.float32,
    )
    return out[0]


def average(block_out, flipped):
    return ((block_out.astype(jnp.float32) + flipped.astype(jnp.float32)) * 0.5).astype(
        jnp.bfloat16
    )


def by_rows(contact_map, w_near, w_far):
    blocks = w_near.shape[0]
    state = lax.all_to_all(contact_map, "cols", split_axis=0, concat_axis=1, tiled=True)
    for block in range(blocks):
        padded = extended(state, ((("rows", "cols"), 0),), NEAR)
        padded = jnp.pad(padded, ((0, 0), (NEAR, NEAR), (0, 0)))
        hidden = jax.nn.relu(valid_conv(padded, w_near[block], NEAR)).astype(jnp.bfloat16)
        padded = extended(hidden, ((("rows", "cols"), 0),), FAR)
        padded = jnp.pad(padded, ((0, 0), (FAR, FAR), (0, 0)))
        block_out = (state.astype(jnp.float32) + valid_conv(padded, w_far[block], FAR)).astype(
            jnp.bfloat16
        )
        mirrored = lax.all_to_all(
            block_out, ("rows", "cols"), split_axis=1, concat_axis=0, tiled=True
        )
        state = average(block_out, jnp.swapaxes(mirrored, 0, 1))
    return lax.all_to_all(state, "cols", split_axis=1, concat_axis=0, tiled=True)


def flip(cells):
    return jnp.transpose(cells, (1, 0, 2))


def tile_kernel(
    count, side, x_ref, near_ref, far_ref, out_ref,
    pads, turned, strips, corners, mirror, hidden, near, far,
    load_sem, send_sem, recv_sem, mirror_sem,
):
    blocks, channels = near_ref.shape[0], near_ref.shape[-1]
    row, col = lax.axis_index("rows"), lax.axis_index("cols")
    last = count - 1
    inner = slice(HALO, HALO + side)
    body = slice(PAD, PAD + side)
    reach = side + 2 * FAR
    span = side + PAD
    half = side // 2

    load = pltpu.make_async_copy(x_ref, pads.at[0, inner, body], load_sem.at[0])
    load.start()

    def there(step):
        di, dj = step
        ok = []
        if di:
            ok.append(row > 0 if di < 0 else row < last)
        if dj:
            ok.append(col > 0 if dj < 0 else col < last)
        return ok[0] if len(ok) == 1 else jnp.logical_and(*ok)

    barrier = pltpu.get_barrier_semaphore()
    friends = (row != col).astype(jnp.int32)

    @pl.when(row != col)
    def _():
        pl.semaphore_signal(
            barrier, inc=1, device_id={"rows": col, "cols": row}, device_id_type=MESH
        )

    for step in SIDES:
        yes = there(step)
        friends += yes.astype(jnp.int32)

        @pl.when(yes)
        def _():
            pl.semaphore_signal(
                barrier, inc=1, device_id={"rows": row + step[0], "cols": col + step[1]},
                device_id_type=MESH,
            )

    def weight_loads(n):
        return (
            pltpu.make_async_copy(near_ref.at[n], near.at[n], load_sem.at[1 + 2 * n]),
            pltpu.make_async_copy(far_ref.at[n], far.at[n], load_sem.at[2 + 2 * n]),
        )

    def clear(ref):
        ref[...] = jnp.zeros(ref.shape, ref.dtype)

    def clear_off_map(ref, height, left, width):
        for at_edge, part in (
            (row == 0, (slice(0, height), slice(None))),
            (row == last, (slice(height + side, height * 2 + side), slice(None))),
            (col == 0, (slice(None), slice(left - width, left))),
            (col == last, (slice(None), slice(left + side, left + side + width))),
        ):
            pl.when(at_edge)(functools.partial(clear, ref.at[part]))

    def rim_copy(n, at):
        di, dj = SIDES[at]
        if di and dj:
            source, target = corners.at[n, 0, at], corners.at[n, 1, at]
        elif di:
            rows = slice(HALO, 2 * HALO) if di < 0 else slice(side, side + HALO)
            to = slice(HALO + side, 2 * HALO + side) if di < 0 else slice(0, HALO)
            source, target = pads.at[n, rows, body], pads.at[n, to, body]
        else:
            source = turned.at[n, slice(0, HALO) if dj < 0 else slice(side - HALO, side)]
            target = strips.at[n, 1 if dj < 0 else 0]
        return pltpu.make_async_remote_copy(
            src_ref=source, dst_ref=target,
            send_sem=send_sem.at[n, at], recv_sem=recv_sem.at[n, at],
            device_id={"rows": row + di, "cols": col + dj}, device_id_type=MESH,
        )

    def rim_start(n, ats):
        for at in ats:
            @pl.when(there(SIDES[at]))
            def _():
                rim_copy(n, at).start()

    def pack_corners(n, cells):
        for at in range(4, 8):
            di, dj = SIDES[at]
            rows = slice(0, HALO) if di < 0 else slice(side - HALO, side)
            bins = slice(0, PACK) if dj < 0 else slice(side - PACK, side)
            corners[n, 0, at] = cells[rows, bins].reshape(HALO * PACK, channels)

    def rim_sent(n):
        for at, step in enumerate(SIDES):
            @pl.when(there(step))
            def _():
                rim_copy(n, at).wait_send()

    def wait_columns(n):
        for at in (2, 3):
            dj = SIDES[at][1]

            @pl.when(there((0, -dj)))
            def _():
                rim_copy(n, at).wait_recv()
                bins = slice(PAD - HALO, PAD) if dj > 0 else slice(
                    PAD + side, PAD + side + HALO)
                pads[n, inner, bins] = flip(strips[n, 0 if dj > 0 else 1])

    def wait_rows(n, above):
        down = above.astype(jnp.int32)
        rows = pl.ds(jnp.where(above, 0, HALO + side), HALO)

        def landed(ref, at):
            pltpu.make_async_remote_copy(
                src_ref=ref, dst_ref=ref,
                send_sem=send_sem.at[n, at], recv_sem=recv_sem.at[n, at],
                device_id={"rows": row, "cols": col}, device_id_type=MESH,
            ).wait_recv()

        @pl.when(jnp.where(above, row, last - row) > 0)
        def _():
            landed(pads.at[n, rows, body], down)
            for right, dj in enumerate((-1, 1)):
                at = 4 + 2 * down + right

                @pl.when(col < last if dj < 0 else col > 0)
                def _():
                    landed(corners.at[n, 1, at], at)
                    bins = slice(PAD - PACK, PAD) if dj > 0 else slice(
                        PAD + side, PAD + side + PACK)
                    pads[n, rows, bins] = corners[n, 1, at].reshape(HALO, PACK, channels)

    def hidden_rows(n, weights, start, size):
        first, wide = PAD - HALO, weights.shape[1]
        shifted = [
            pads[n, pl.ds(start, size + 2 * NEAR), first + NEAR * b:first + NEAR * b + span]
            for b in range(3)
        ]
        taps = [
            shifted[b][NEAR * a:NEAR * a + size].reshape(size * span, channels)
            for a in range(3) for b in range(3)
        ]
        total = jnp.dot(
            jnp.concatenate(taps, axis=1), weights, preferred_element_type=jnp.float32
        )
        hidden[pl.ds(start, size), :, :wide] = (
            jnp.maximum(total, 0.0).astype(hidden.dtype).reshape(size, span, wide)
        )

    def block_out_of(n, lane, weights, start):
        lanes = slice(lane * channels, (lane + 1) * channels)
        shifted = [
            hidden[pl.ds(start, half + 2 * FAR), FAR * b:FAR * b + side, lanes]
            for b in range(3)
        ]
        taps = [
            shifted[b][FAR * a:FAR * a + half].reshape(half * side, channels)
            for a in range(3) for b in range(3)
        ]
        total = jnp.dot(
            jnp.concatenate(taps, axis=1), weights, preferred_element_type=jnp.float32
        ).reshape(half, side, channels)
        own = pads[n, pl.ds(HALO + start, half), body]
        return (own.astype(jnp.float32) + total).astype(jnp.bfloat16)

    def halves_of(n, weights, half_done):
        wait_columns(n)
        for copy in weight_loads(n):
            copy.wait()
        middle = -(-(side - 2 * NEAR) // HALO)

        @pl.loop(0, middle + 2)
        def _(step):
            k = step - middle
            above = lax.rem(row, 2) == 1 - k

            @pl.when(k >= 0)
            def _():
                wait_rows(n, above)

            between = jnp.minimum(HALO * (step + 1), reach - 2 * HALO)
            ends = jnp.where(above, 0, reach - HALO)
            hidden_rows(n, weights(), jnp.where(k < 0, between, ends), HALO)

            @pl.when(k >= 0)
            def _():
                clear_off_map(hidden, FAR, FAR, FAR)
                half_done(k, jnp.where(above, 0, half))

    def straight(w, n):
        return w[n].reshape(9 * channels, channels)

    def crossed(w, n):
        return jnp.concatenate([w[n, b, a] for a in range(3) for b in range(3)], axis=0)

    for n in range(blocks):
        clear_off_map(pads.at[n], HALO, PAD, PAD)

    def swap(k, start):
        part = pl.ds(start, half)
        return pltpu.make_async_remote_copy(
            src_ref=mirror.at[0, part], dst_ref=mirror.at[1, part],
            send_sem=mirror_sem.at[0, k], recv_sem=mirror_sem.at[1, k],
            device_id={"rows": col, "cols": row}, device_id_type=MESH,
        )

    def mirror_half(k, start):
        part = pl.ds(start, half)
        mirror[0, part] = block_out_of(0, 0, straight(far, 0), start)

        @pl.when(row != col)
        def _():
            swap(k, start).start()

        @pl.when(row == col)
        def _():
            mirror[1, part] = mirror[0, part]

    def columns_half(n, k):
        end = jnp.where(lax.rem(col, 2) == 1 - k, 0, 1)
        part = pl.ds(end * half, half)

        @pl.when(row != col)
        def _():
            swap(k, end * half).wait_recv()

        turned[n, part] = average(turned[n, part], mirror[1, part])
        for at in (2, 3):
            pl.when(end == at - 2)(functools.partial(rim_start, n, (at,)))

    def average_half(n, k, start):
        value = average(
            block_out_of(n, 0, straight(far, n), start),
            block_out_of(n, 1, crossed(far, n), start),
        )
        if n == blocks - 1:
            out_ref[pl.ds(start, half)] = value
        else:
            pads[n + 1, pl.ds(HALO + start, half), body] = value

    def mirror_sent():
        @pl.when(row != col)
        def _():
            for k in range(2):
                swap(k, jnp.where(lax.rem(row, 2) == 1 - k, 0, half)).wait_send()

    load.wait()
    for copy in weight_loads(0):
        copy.start()
    state = pads[0, inner, body]
    turned[0] = flip(state)
    pack_corners(0, state)
    pl.semaphore_wait(barrier, friends)
    rim_start(0, (2, 3, 0, 1, 4, 5, 6, 7))

    for n in range(blocks):
        if n == 0:
            halves_of(n, lambda: straight(near, n), mirror_half)
            for copy in weight_loads(n + 1):
                copy.start()
            turned[n + 1] = flip(mirror[0])
            rim_sent(n)
            pl.loop(0, 2)(functools.partial(columns_half, n + 1))
            state = flip(turned[n + 1])
            pads[n + 1, inner, body] = state
            rim_start(n + 1, (0, 1))
            pack_corners(n + 1, state)
            rim_start(n + 1, (4, 5, 6, 7))
            mirror_sent()
        else:
            halves_of(
                n, lambda: jnp.concatenate([straight(near, n), crossed(near, n)], axis=1),
                functools.partial(average_half, n),
            )
            rim_sent(n)
            if n < blocks - 1:
                for copy in weight_loads(n + 1):
                    copy.start()
                state = pads[n + 1, inner, body]
                turned[n + 1] = flip(state)
                pack_corners(n + 1, state)
                rim_start(n + 1, (2, 3, 0, 1, 4, 5, 6, 7))


def by_tiles(contact_map, w_near, w_far):
    blocks, channels = w_near.shape[0], w_near.shape[-1]
    side, count = contact_map.shape[0], lax.axis_size("rows")
    kind = contact_map.dtype
    return pl.pallas_call(
        functools.partial(tile_kernel, count, side),
        out_shape=jax.ShapeDtypeStruct(contact_map.shape, kind),
        in_specs=[pl.BlockSpec(memory_space=pltpu.HBM)] * 3,
        out_specs=pl.BlockSpec(memory_space=pltpu.VMEM),
        scratch_shapes=[
            pltpu.VMEM((blocks, side + 2 * HALO, side + 2 * PAD, channels), kind),
            pltpu.VMEM((blocks, side, side, channels), kind),
            pltpu.VMEM((blocks, 2, HALO, side, channels), kind),
            pltpu.VMEM((blocks, 2, len(SIDES), HALO * PACK, channels), kind),
            pltpu.VMEM((2, side, side, channels), kind),
            pltpu.VMEM((side + 2 * FAR, side + PAD, 2 * channels), kind),
            pltpu.VMEM(w_near.shape, kind),
            pltpu.VMEM(w_far.shape, kind),
            pltpu.SemaphoreType.DMA((1 + 2 * blocks,)),
            pltpu.SemaphoreType.DMA((blocks, len(SIDES))),
            pltpu.SemaphoreType.DMA((blocks, len(SIDES))),
            pltpu.SemaphoreType.DMA((2, 2)),
        ],
        compiler_params=pltpu.CompilerParams(
            collective_id=0, has_side_effects=True, vmem_limit_bytes=431 * 2**17
        ),
    )(contact_map, w_near, w_far)


def on_device(contact_map, w_near, w_far):
    side = contact_map.shape[0]
    square = side == contact_map.shape[1] and side % PAD == 0
    if square and lax.axis_size("rows") == lax.axis_size("cols") and w_near.shape[0] > 1:
        return by_tiles(contact_map, w_near, w_far)
    return by_rows(contact_map, w_near, w_far)


def solution(mesh):
    in_specs = (P(("groups", "rows"), "cols", None), P(), P())
    out_specs = P(("groups", "rows"), "cols", None)
    return jax.shard_map(
        on_device, mesh=mesh, in_specs=in_specs, out_specs=out_specs, check_vma=False
    )
```

```python
import functools

import jax
import jax.numpy as jnp
from jax import lax
from jax.experimental import pallas as pl
from jax.experimental.pallas import tpu as pltpu
from jax.sharding import PartitionSpec as P

MESH = pl.DeviceIdType.MESH
NEAR, FAR = 2, 4
HALO = NEAR + FAR
PAD, PACK = 16, 8
SIDES = [(-1, 0), (1, 0), (0, -1), (0, 1), (-1, -1), (-1, 1), (1, -1), (1, 1)]


def extended(cells, sides, width):
    for axis, dim in sides:
        count = lax.axis_size(axis)
        ends = count - 1
        head = lax.slice_in_dim(cells, 0, width, axis=dim)
        tail = lax.slice_in_dim(cells, cells.shape[dim] - width, cells.shape[dim], axis=dim)
        cells = jnp.concatenate(
            [
                lax.ppermute(tail, axis, [(i, (i + 1) % count) for i in range(ends)]),
                cells,
                lax.ppermute(head, axis, [((i + 1) % count, i) for i in range(ends)]),
            ],
            axis=dim,
        )
    return cells


def valid_conv(padded, kernel, spread):
    out = lax.conv_general_dilated(
        padded[None],
        kernel,
        (1, 1),
        "VALID",
        rhs_dilation=(spread, spread),
        dimension_numbers=("NHWC", "HWIO", "NHWC"),
        preferred_element_type=jnp.float32,
    )
    return out[0]


def average(block_out, flipped):
    return ((block_out.astype(jnp.float32) + flipped.astype(jnp.float32)) * 0.5).astype(
        jnp.bfloat16
    )


def by_rows(contact_map, w_near, w_far):
    blocks = w_near.shape[0]
    state = lax.all_to_all(contact_map, "cols", split_axis=0, concat_axis=1, tiled=True)
    for block in range(blocks):
        padded = extended(state, ((("rows", "cols"), 0),), NEAR)
        padded = jnp.pad(padded, ((0, 0), (NEAR, NEAR), (0, 0)))
        hidden = jax.nn.relu(valid_conv(padded, w_near[block], NEAR)).astype(jnp.bfloat16)
        padded = extended(hidden, ((("rows", "cols"), 0),), FAR)
        padded = jnp.pad(padded, ((0, 0), (FAR, FAR), (0, 0)))
        block_out = (state.astype(jnp.float32) + valid_conv(padded, w_far[block], FAR)).astype(
            jnp.bfloat16
        )
        mirrored = lax.all_to_all(
            block_out, ("rows", "cols"), split_axis=1, concat_axis=0, tiled=True
        )
        state = average(block_out, jnp.swapaxes(mirrored, 0, 1))
    return lax.all_to_all(state, "cols", split_axis=1, concat_axis=0, tiled=True)


def flip(cells):
    return jnp.transpose(cells, (1, 0, 2))


def tile_kernel(
    count, side, x_ref, near_ref, far_ref, out_ref,
    pads, turned, strips, corners, mirror, hidden, near, far,
    load_sem, send_sem, recv_sem, mirror_sem,
):
    blocks, channels = near_ref.shape[0], near_ref.shape[-1]
    row, col = lax.axis_index("rows"), lax.axis_index("cols")
    last = count - 1
    inner = slice(HALO, HALO + side)
    body = slice(PAD, PAD + side)
    reach = side + 2 * FAR
    span = side + PAD
    half = side // 2

    load = pltpu.make_async_copy(x_ref, pads.at[0, inner, body], load_sem.at[0])
    load.start()

    def there(step):
        di, dj = step
        ok = []
        if di:
            ok.append(row > 0 if di < 0 else row < last)
        if dj:
            ok.append(col > 0 if dj < 0 else col < last)
        return ok[0] if len(ok) == 1 else jnp.logical_and(*ok)

    barrier = pltpu.get_barrier_semaphore()
    friends = (row != col).astype(jnp.int32)

    @pl.when(row != col)
    def _():
        pl.semaphore_signal(
            barrier, inc=1, device_id={"rows": col, "cols": row}, device_id_type=MESH
        )

    for step in SIDES:
        yes = there(step)
        friends += yes.astype(jnp.int32)

        @pl.when(yes)
        def _():
            pl.semaphore_signal(
                barrier, inc=1, device_id={"rows": row + step[0], "cols": col + step[1]},
                device_id_type=MESH,
            )

    def weight_loads(n):
        return (
            pltpu.make_async_copy(near_ref.at[n], near.at[n], load_sem.at[1 + 2 * n]),
            pltpu.make_async_copy(far_ref.at[n], far.at[n], load_sem.at[2 + 2 * n]),
        )

    def clear(ref):
        ref[...] = jnp.zeros(ref.shape, ref.dtype)

    def clear_off_map(ref, height, left, width):
        for at_edge, part in (
            (row == 0, (slice(0, height), slice(None))),
            (row == last, (slice(height + side, height * 2 + side), slice(None))),
            (col == 0, (slice(None), slice(left - width, left))),
            (col == last, (slice(None), slice(left + side, left + side + width))),
        ):
            pl.when(at_edge)(functools.partial(clear, ref.at[part]))

    def rim_copy(n, at):
        di, dj = SIDES[at]
        if di and dj:
            source, target = corners.at[n, 0, at], corners.at[n, 1, at]
        elif di:
            rows = slice(HALO, 2 * HALO) if di < 0 else slice(side, side + HALO)
            to = slice(HALO + side, 2 * HALO + side) if di < 0 else slice(0, HALO)
            source, target = pads.at[n, rows, body], pads.at[n, to, body]
        else:
            source = turned.at[n, slice(0, HALO) if dj < 0 else slice(side - HALO, side)]
            target = strips.at[n, 1 if dj < 0 else 0]
        return pltpu.make_async_remote_copy(
            src_ref=source, dst_ref=target,
            send_sem=send_sem.at[n, at], recv_sem=recv_sem.at[n, at],
            device_id={"rows": row + di, "cols": col + dj}, device_id_type=MESH,
        )

    def rim_start(n, ats):
        for at in ats:
            @pl.when(there(SIDES[at]))
            def _():
                rim_copy(n, at).start()

    def pack_corners(n, end):
        bins = slice(0, HALO) if end == 0 else slice(side - HALO, side)
        for at in (4 + end, 6 + end):
            rows = slice(0, PACK) if SIDES[at][0] < 0 else slice(side - PACK, side)
            corners[n, 0, at] = turned[n, bins, rows].reshape(HALO * PACK, channels)

    def rim_sent(n):
        for at, step in enumerate(SIDES):
            @pl.when(there(step))
            def _():
                rim_copy(n, at).wait_send()

    def wait_columns(n):
        for at in (2, 3):
            dj = SIDES[at][1]

            @pl.when(there((0, -dj)))
            def _():
                rim_copy(n, at).wait_recv()
                bins = slice(PAD - HALO, PAD) if dj > 0 else slice(
                    PAD + side, PAD + side + HALO)
                pads[n, inner, bins] = flip(strips[n, 0 if dj > 0 else 1])

    def wait_rows(n, above):
        down = above.astype(jnp.int32)
        rows = pl.ds(jnp.where(above, 0, HALO + side), HALO)

        def landed(ref, at):
            pltpu.make_async_remote_copy(
                src_ref=ref, dst_ref=ref,
                send_sem=send_sem.at[n, at], recv_sem=recv_sem.at[n, at],
                device_id={"rows": row, "cols": col}, device_id_type=MESH,
            ).wait_recv()

        @pl.when(jnp.where(above, row, last - row) > 0)
        def _():
            landed(pads.at[n, rows, body], down)
            for right, dj in enumerate((-1, 1)):
                at = 4 + 2 * down + right

                @pl.when(col < last if dj < 0 else col > 0)
                def _():
                    landed(corners.at[n, 1, at], at)
                    bins = slice(PAD - HALO, PAD) if dj > 0 else slice(
                        PAD + side, PAD + side + HALO)
                    corner = flip(corners[n, 1, at].reshape(HALO, PACK, channels))
                    pads[n, rows, bins] = jnp.where(
                        above, corner[PACK - HALO:], corner[:HALO])

    def hidden_rows(n, weights, start, size):
        first, wide = PAD - HALO, weights.shape[1]
        shifted = [
            pads[n, pl.ds(start, size + 2 * NEAR), first + NEAR * b:first + NEAR * b + span]
            for b in range(3)
        ]
        taps = [
            shifted[b][NEAR * a:NEAR * a + size].reshape(size * span, channels)
            for a in range(3) for b in range(3)
        ]
        total = jnp.dot(
            jnp.concatenate(taps, axis=1), weights, preferred_element_type=jnp.float32
        )
        hidden[pl.ds(start, size), :, :wide] = (
            jnp.maximum(total, 0.0).astype(hidden.dtype).reshape(size, span, wide)
        )

    def block_out_of(n, lane, weights, start):
        lanes = slice(lane * channels, (lane + 1) * channels)
        shifted = [
            hidden[pl.ds(start, half + 2 * FAR), FAR * b:FAR * b + side, lanes]
            for b in range(3)
        ]
        taps = [
            shifted[b][FAR * a:FAR * a + half].reshape(half * side, channels)
            for a in range(3) for b in range(3)
        ]
        total = jnp.dot(
            jnp.concatenate(taps, axis=1), weights, preferred_element_type=jnp.float32
        ).reshape(half, side, channels)
        own = pads[n, pl.ds(HALO + start, half), body]
        return (own.astype(jnp.float32) + total).astype(jnp.bfloat16)

    def halves_of(n, weights, half_done):
        wait_columns(n)
        for copy in weight_loads(n):
            copy.wait()
        middle = -(-(side - 2 * NEAR) // HALO)

        @pl.loop(0, middle + 2)
        def _(step):
            k = step - middle
            above = lax.rem(row, 2) == 1 - k

            @pl.when(k >= 0)
            def _():
                wait_rows(n, above)

            between = jnp.minimum(HALO * (step + 1), reach - 2 * HALO)
            ends = jnp.where(above, 0, reach - HALO)
            hidden_rows(n, weights(), jnp.where(k < 0, between, ends), HALO)

            @pl.when(k >= 0)
            def _():
                clear_off_map(hidden, FAR, FAR, FAR)
                half_done(k, jnp.where(above, 0, half))

    def straight(w, n):
        return w[n].reshape(9 * channels, channels)

    def crossed(w, n):
        return jnp.concatenate([w[n, b, a] for a in range(3) for b in range(3)], axis=0)

    for n in range(blocks):
        clear_off_map(pads.at[n], HALO, PAD, PAD)

    def swap(k, start):
        part = pl.ds(start, half)
        return pltpu.make_async_remote_copy(
            src_ref=mirror.at[0, part], dst_ref=mirror.at[1, part],
            send_sem=mirror_sem.at[0, k], recv_sem=mirror_sem.at[1, k],
            device_id={"rows": col, "cols": row}, device_id_type=MESH,
        )

    def mirror_half(k, start):
        part = pl.ds(start, half)
        mirror[0, part] = block_out_of(0, 0, straight(far, 0), start)

        @pl.when(row != col)
        def _():
            swap(k, start).start()

        @pl.when(row == col)
        def _():
            mirror[1, part] = mirror[0, part]

    def columns_half(n, k):
        end = jnp.where(lax.rem(col, 2) == 1 - k, 0, 1)
        part = pl.ds(end * half, half)

        @pl.when(row != col)
        def _():
            swap(k, end * half).wait_recv()

        turned[n, part] = average(turned[n, part], mirror[1, part])
        for which in range(2):
            @pl.when(end == which)
            def _():
                rim_start(n, (2 + which,))
                pack_corners(n, which)
                rim_start(n, (4 + which, 6 + which))

    def average_half(n, k, start):
        value = average(
            block_out_of(n, 0, straight(far, n), start),
            block_out_of(n, 1, crossed(far, n), start),
        )
        if n == blocks - 1:
            out_ref[pl.ds(start, half)] = value
        else:
            pads[n + 1, pl.ds(HALO + start, half), body] = value

    def mirror_sent():
        @pl.when(row != col)
        def _():
            for k in range(2):
                swap(k, jnp.where(lax.rem(row, 2) == 1 - k, 0, half)).wait_send()

    load.wait()
    for copy in weight_loads(0):
        copy.start()
    state = pads[0, inner, body]
    turned[0] = flip(state)
    pack_corners(0, 0)
    pack_corners(0, 1)
    pl.semaphore_wait(barrier, friends)
    rim_start(0, (2, 3, 0, 1, 4, 5, 6, 7))

    for n in range(blocks):
        if n == 0:
            halves_of(n, lambda: straight(near, n), mirror_half)
            for copy in weight_loads(n + 1):
                copy.start()
            turned[n + 1] = flip(mirror[0])
            rim_sent(n)
            pl.loop(0, 2)(functools.partial(columns_half, n + 1))
            state = flip(turned[n + 1])
            pads[n + 1, inner, body] = state
            rim_start(n + 1, (0, 1))
            mirror_sent()
        else:
            halves_of(
                n, lambda: jnp.concatenate([straight(near, n), crossed(near, n)], axis=1),
                functools.partial(average_half, n),
            )
            rim_sent(n)
            if n < blocks - 1:
                for copy in weight_loads(n + 1):
                    copy.start()
                state = pads[n + 1, inner, body]
                turned[n + 1] = flip(state)
                pack_corners(n + 1, 0)
                pack_corners(n + 1, 1)
                rim_start(n + 1, (2, 3, 0, 1, 4, 5, 6, 7))


def by_tiles(contact_map, w_near, w_far):
    blocks, channels = w_near.shape[0], w_near.shape[-1]
    side, count = contact_map.shape[0], lax.axis_size("rows")
    kind = contact_map.dtype
    return pl.pallas_call(
        functools.partial(tile_kernel, count, side),
        out_shape=jax.ShapeDtypeStruct(contact_map.shape, kind),
        in_specs=[pl.BlockSpec(memory_space=pltpu.HBM)] * 3,
        out_specs=pl.BlockSpec(memory_space=pltpu.VMEM),
        scratch_shapes=[
            pltpu.VMEM((blocks, side + 2 * HALO, side + 2 * PAD, channels), kind),
            pltpu.VMEM((blocks, side, side, channels), kind),
            pltpu.VMEM((blocks, 2, HALO, side, channels), kind),
            pltpu.VMEM((blocks, 2, len(SIDES), HALO * PACK, channels), kind),
            pltpu.VMEM((2, side, side, channels), kind),
            pltpu.VMEM((side + 2 * FAR, side + PAD, 2 * channels), kind),
            pltpu.VMEM(w_near.shape, kind),
            pltpu.VMEM(w_far.shape, kind),
            pltpu.SemaphoreType.DMA((1 + 2 * blocks,)),
            pltpu.SemaphoreType.DMA((blocks, len(SIDES))),
            pltpu.SemaphoreType.DMA((blocks, len(SIDES))),
            pltpu.SemaphoreType.DMA((2, 2)),
        ],
        compiler_params=pltpu.CompilerParams(
            collective_id=0, has_side_effects=True, vmem_limit_bytes=431 * 2**17
        ),
    )(contact_map, w_near, w_far)


def on_device(contact_map, w_near, w_far):
    side = contact_map.shape[0]
    square = side == contact_map.shape[1] and side % PAD == 0
    if square and lax.axis_size("rows") == lax.axis_size("cols") and w_near.shape[0] > 1:
        return by_tiles(contact_map, w_near, w_far)
    return by_rows(contact_map, w_near, w_far)


def solution(mesh):
    in_specs = (P(("groups", "rows"), "cols", None), P(), P())
    out_specs = P(("groups", "rows"), "cols", None)
    return jax.shard_map(
        on_device, mesh=mesh, in_specs=in_specs, out_specs=out_specs, check_vma=False
    )
```

```python
import functools

import jax
import jax.numpy as jnp
from jax import lax
from jax.experimental import pallas as pl
from jax.experimental.pallas import tpu as pltpu
from jax.sharding import PartitionSpec as P

MESH = pl.DeviceIdType.MESH
NEAR, FAR = 2, 4
HALO = NEAR + FAR
PAD, PACK = 16, 8
SIDES = [(-1, 0), (1, 0), (0, -1), (0, 1), (-1, -1), (-1, 1), (1, -1), (1, 1)]


def extended(cells, sides, width):
    for axis, dim in sides:
        count = lax.axis_size(axis)
        ends = count - 1
        head = lax.slice_in_dim(cells, 0, width, axis=dim)
        tail = lax.slice_in_dim(cells, cells.shape[dim] - width, cells.shape[dim], axis=dim)
        cells = jnp.concatenate(
            [
                lax.ppermute(tail, axis, [(i, (i + 1) % count) for i in range(ends)]),
                cells,
                lax.ppermute(head, axis, [((i + 1) % count, i) for i in range(ends)]),
            ],
            axis=dim,
        )
    return cells


def valid_conv(padded, kernel, spread):
    out = lax.conv_general_dilated(
        padded[None],
        kernel,
        (1, 1),
        "VALID",
        rhs_dilation=(spread, spread),
        dimension_numbers=("NHWC", "HWIO", "NHWC"),
        preferred_element_type=jnp.float32,
    )
    return out[0]


def average(block_out, flipped):
    return ((block_out.astype(jnp.float32) + flipped.astype(jnp.float32)) * 0.5).astype(
        jnp.bfloat16
    )


def by_rows(contact_map, w_near, w_far):
    blocks = w_near.shape[0]
    state = lax.all_to_all(contact_map, "cols", split_axis=0, concat_axis=1, tiled=True)
    for block in range(blocks):
        padded = extended(state, ((("rows", "cols"), 0),), NEAR)
        padded = jnp.pad(padded, ((0, 0), (NEAR, NEAR), (0, 0)))
        hidden = jax.nn.relu(valid_conv(padded, w_near[block], NEAR)).astype(jnp.bfloat16)
        padded = extended(hidden, ((("rows", "cols"), 0),), FAR)
        padded = jnp.pad(padded, ((0, 0), (FAR, FAR), (0, 0)))
        block_out = (state.astype(jnp.float32) + valid_conv(padded, w_far[block], FAR)).astype(
            jnp.bfloat16
        )
        mirrored = lax.all_to_all(
            block_out, ("rows", "cols"), split_axis=1, concat_axis=0, tiled=True
        )
        state = average(block_out, jnp.swapaxes(mirrored, 0, 1))
    return lax.all_to_all(state, "cols", split_axis=1, concat_axis=0, tiled=True)


def flip(cells):
    return jnp.transpose(cells, (1, 0, 2))


def tile_kernel(
    count, side, x_ref, near_ref, far_ref, out_ref,
    pads, turned, strips, corners, mirror, hidden, near, far,
    load_sem, send_sem, recv_sem, mirror_sem,
):
    blocks, channels = near_ref.shape[0], near_ref.shape[-1]
    row, col = lax.axis_index("rows"), lax.axis_index("cols")
    last = count - 1
    inner = slice(HALO, HALO + side)
    body = slice(PAD, PAD + side)
    reach = side + 2 * FAR
    span = side + PAD
    half = side // 2

    load = pltpu.make_async_copy(x_ref, pads.at[0, inner, body], load_sem.at[0])
    load.start()

    def there(step):
        di, dj = step
        ok = []
        if di:
            ok.append(row > 0 if di < 0 else row < last)
        if dj:
            ok.append(col > 0 if dj < 0 else col < last)
        return ok[0] if len(ok) == 1 else jnp.logical_and(*ok)

    barrier = pltpu.get_barrier_semaphore()
    friends = (row != col).astype(jnp.int32)

    @pl.when(row != col)
    def _():
        pl.semaphore_signal(
            barrier, inc=1, device_id={"rows": col, "cols": row}, device_id_type=MESH
        )

    for step in SIDES:
        yes = there(step)
        friends += yes.astype(jnp.int32)

        @pl.when(yes)
        def _():
            pl.semaphore_signal(
                barrier, inc=1, device_id={"rows": row + step[0], "cols": col + step[1]},
                device_id_type=MESH,
            )

    def weight_loads(n):
        return (
            pltpu.make_async_copy(near_ref.at[n], near.at[n], load_sem.at[1 + 2 * n]),
            pltpu.make_async_copy(far_ref.at[n], far.at[n], load_sem.at[2 + 2 * n]),
        )

    def clear(ref):
        ref[...] = jnp.zeros(ref.shape, ref.dtype)

    def clear_off_map(ref, height, left, width):
        for at_edge, part in (
            (row == 0, (slice(0, height), slice(None))),
            (row == last, (slice(height + side, height * 2 + side), slice(None))),
            (col == 0, (slice(None), slice(left - width, left))),
            (col == last, (slice(None), slice(left + side, left + side + width))),
        ):
            pl.when(at_edge)(functools.partial(clear, ref.at[part]))

    def rim_copy(n, at):
        di, dj = SIDES[at]
        if di and dj:
            source, target = corners.at[n, 0, at], corners.at[n, 1, at]
        elif di:
            rows = slice(HALO, 2 * HALO) if di < 0 else slice(side, side + HALO)
            to = slice(HALO + side, 2 * HALO + side) if di < 0 else slice(0, HALO)
            source, target = pads.at[n, rows, body], pads.at[n, to, body]
        else:
            source = turned.at[n, slice(0, HALO) if dj < 0 else slice(side - HALO, side)]
            target = strips.at[n, 1 if dj < 0 else 0]
        return pltpu.make_async_remote_copy(
            src_ref=source, dst_ref=target,
            send_sem=send_sem.at[n, at], recv_sem=recv_sem.at[n, at],
            device_id={"rows": row + di, "cols": col + dj}, device_id_type=MESH,
        )

    def rim_start(n, ats):
        for at in ats:
            @pl.when(there(SIDES[at]))
            def _():
                rim_copy(n, at).start()

    def pack_corners(n, end):
        bins = slice(0, HALO) if end == 0 else slice(side - HALO, side)
        for at in (4 + end, 6 + end):
            rows = slice(0, PACK) if SIDES[at][0] < 0 else slice(side - PACK, side)
            corners[n, 0, at] = turned[n, bins, rows].reshape(HALO * PACK, channels)

    def rim_sent(n):
        for at, step in enumerate(SIDES):
            @pl.when(there(step))
            def _():
                rim_copy(n, at).wait_send()

    def wait_columns(n):
        for at in (2, 3):
            dj = SIDES[at][1]

            @pl.when(there((0, -dj)))
            def _():
                rim_copy(n, at).wait_recv()
                bins = slice(PAD - HALO, PAD) if dj > 0 else slice(
                    PAD + side, PAD + side + HALO)
                pads[n, inner, bins] = flip(strips[n, 0 if dj > 0 else 1])

    def wait_rows(n, above):
        down = above.astype(jnp.int32)
        rows = pl.ds(jnp.where(above, 0, HALO + side), HALO)

        def landed(ref, at):
            pltpu.make_async_remote_copy(
                src_ref=ref, dst_ref=ref,
                send_sem=send_sem.at[n, at], recv_sem=recv_sem.at[n, at],
                device_id={"rows": row, "cols": col}, device_id_type=MESH,
            ).wait_recv()

        @pl.when(jnp.where(above, row, last - row) > 0)
        def _():
            landed(pads.at[n, rows, body], down)
            for right, dj in enumerate((-1, 1)):
                at = 4 + 2 * down + right

                @pl.when(col < last if dj < 0 else col > 0)
                def _():
                    landed(corners.at[n, 1, at], at)
                    bins = slice(PAD - HALO, PAD) if dj > 0 else slice(
                        PAD + side, PAD + side + HALO)
                    corner = flip(corners[n, 1, at].reshape(HALO, PACK, channels))
                    pads[n, rows, bins] = jnp.where(
                        above, corner[PACK - HALO:], corner[:HALO])

    def hidden_rows(n, weights, start, size):
        first, wide = PAD - HALO, weights.shape[1]
        shifted = [
            pads[n, pl.ds(start, size + 2 * NEAR), first + NEAR * b:first + NEAR * b + span]
            for b in range(3)
        ]
        taps = [
            shifted[b][NEAR * a:NEAR * a + size].reshape(size * span, channels)
            for a in range(3) for b in range(3)
        ]
        total = jnp.dot(
            jnp.concatenate(taps, axis=1), weights, preferred_element_type=jnp.float32
        )
        hidden[pl.ds(start, size), :, :wide] = (
            jnp.maximum(total, 0.0).astype(hidden.dtype).reshape(size, span, wide)
        )

    def block_out_of(n, lane, weights, start):
        lanes = slice(lane * channels, (lane + 1) * channels)
        shifted = [
            hidden[pl.ds(start, half + 2 * FAR), FAR * b:FAR * b + side, lanes]
            for b in range(3)
        ]
        taps = [
            shifted[b][FAR * a:FAR * a + half].reshape(half * side, channels)
            for a in range(3) for b in range(3)
        ]
        total = jnp.dot(
            jnp.concatenate(taps, axis=1), weights, preferred_element_type=jnp.float32
        ).reshape(half, side, channels)
        own = pads[n, pl.ds(HALO + start, half), body]
        return (own.astype(jnp.float32) + total).astype(jnp.bfloat16)

    def halves_of(n, weights, half_done):
        wait_columns(n)
        for copy in weight_loads(n):
            copy.wait()
        middle = -(-(side - 2 * NEAR) // HALO)

        @pl.loop(0, middle + 2)
        def _(step):
            k = step - middle
            above = lax.rem(row, 2) == 1 - k

            @pl.when(k >= 0)
            def _():
                wait_rows(n, above)

            between = jnp.minimum(HALO * (step + 1), reach - 2 * HALO)
            ends = jnp.where(above, 0, reach - HALO)
            hidden_rows(n, weights(), jnp.where(k < 0, between, ends), HALO)

            @pl.when(k >= 0)
            def _():
                clear_off_map(hidden, FAR, FAR, FAR)
                half_done(k, jnp.where(above, 0, half))

    def straight(w, n):
        return w[n].reshape(9 * channels, channels)

    def crossed(w, n):
        return jnp.concatenate([w[n, b, a] for a in range(3) for b in range(3)], axis=0)

    for n in range(blocks):
        clear_off_map(pads.at[n], HALO, PAD, PAD)

    def swap(k, start):
        part = pl.ds(start, half)
        return pltpu.make_async_remote_copy(
            src_ref=mirror.at[0, part], dst_ref=mirror.at[1, part],
            send_sem=mirror_sem.at[0, k], recv_sem=mirror_sem.at[1, k],
            device_id={"rows": col, "cols": row}, device_id_type=MESH,
        )

    def mirror_half(k, start):
        part = pl.ds(start, half)
        mirror[0, part] = block_out_of(0, 0, straight(far, 0), start)

        @pl.when(row != col)
        def _():
            swap(k, start).start()

        @pl.when(row == col)
        def _():
            mirror[1, part] = mirror[0, part]

    def end_of(k):
        return jnp.where(lax.rem(col, 2) == 1 - k, 0, 1)

    def columns_half(n, k):
        part = pl.ds(end_of(k) * half, half)

        @pl.when(row != col)
        def _():
            swap(k, end_of(k) * half).wait_recv()

        turned[n, part] = average(turned[n, part], mirror[1, part])

    def send_end(n, end):
        for which in range(2):
            @pl.when(end == which)
            def _():
                rim_start(n, (2 + which,))
                pack_corners(n, which)
                rim_start(n, (4 + which, 6 + which))

    def average_half(n, k, start):
        value = average(
            block_out_of(n, 0, straight(far, n), start),
            block_out_of(n, 1, crossed(far, n), start),
        )
        if n == blocks - 1:
            out_ref[pl.ds(start, half)] = value
        else:
            pads[n + 1, pl.ds(HALO + start, half), body] = value

    def mirror_sent():
        @pl.when(row != col)
        def _():
            for k in range(2):
                swap(k, jnp.where(lax.rem(row, 2) == 1 - k, 0, half)).wait_send()

    load.wait()
    for copy in weight_loads(0):
        copy.start()
    state = pads[0, inner, body]
    turned[0] = flip(state)
    pack_corners(0, 0)
    pack_corners(0, 1)
    pl.semaphore_wait(barrier, friends)
    rim_start(0, (2, 3, 0, 1, 4, 5, 6, 7))

    for n in range(blocks):
        if n == 0:
            halves_of(n, lambda: straight(near, n), mirror_half)
            for copy in weight_loads(n + 1):
                copy.start()
            turned[n + 1] = flip(mirror[0])
            rim_sent(n)
            columns_half(n + 1, 0)
            send_end(n + 1, end_of(0))
            columns_half(n + 1, 1)
            state = flip(turned[n + 1])
            pads[n + 1, inner, body] = state
            rim_start(n + 1, (0, 1))
            send_end(n + 1, end_of(1))
            mirror_sent()
        else:
            halves_of(
                n, lambda: jnp.concatenate([straight(near, n), crossed(near, n)], axis=1),
                functools.partial(average_half, n),
            )
            rim_sent(n)
            if n < blocks - 1:
                for copy in weight_loads(n + 1):
                    copy.start()
                state = pads[n + 1, inner, body]
                turned[n + 1] = flip(state)
                pack_corners(n + 1, 0)
                pack_corners(n + 1, 1)
                rim_start(n + 1, (2, 3, 0, 1, 4, 5, 6, 7))


def by_tiles(contact_map, w_near, w_far):
    blocks, channels = w_near.shape[0], w_near.shape[-1]
    side, count = contact_map.shape[0], lax.axis_size("rows")
    kind = contact_map.dtype
    return pl.pallas_call(
        functools.partial(tile_kernel, count, side),
        out_shape=jax.ShapeDtypeStruct(contact_map.shape, kind),
        in_specs=[pl.BlockSpec(memory_space=pltpu.HBM)] * 3,
        out_specs=pl.BlockSpec(memory_space=pltpu.VMEM),
        scratch_shapes=[
            pltpu.VMEM((blocks, side + 2 * HALO, side + 2 * PAD, channels), kind),
            pltpu.VMEM((blocks, side, side, channels), kind),
            pltpu.VMEM((blocks, 2, HALO, side, channels), kind),
            pltpu.VMEM((blocks, 2, len(SIDES), HALO * PACK, channels), kind),
            pltpu.VMEM((2, side, side, channels), kind),
            pltpu.VMEM((side + 2 * FAR, side + PAD, 2 * channels), kind),
            pltpu.VMEM(w_near.shape, kind),
            pltpu.VMEM(w_far.shape, kind),
            pltpu.SemaphoreType.DMA((1 + 2 * blocks,)),
            pltpu.SemaphoreType.DMA((blocks, len(SIDES))),
            pltpu.SemaphoreType.DMA((blocks, len(SIDES))),
            pltpu.SemaphoreType.DMA((2, 2)),
        ],
        compiler_params=pltpu.CompilerParams(
            collective_id=0, has_side_effects=True, vmem_limit_bytes=431 * 2**17
        ),
    )(contact_map, w_near, w_far)


def on_device(contact_map, w_near, w_far):
    side = contact_map.shape[0]
    square = side == contact_map.shape[1] and side % PAD == 0
    if square and lax.axis_size("rows") == lax.axis_size("cols") and w_near.shape[0] > 1:
        return by_tiles(contact_map, w_near, w_far)
    return by_rows(contact_map, w_near, w_far)


def solution(mesh):
    in_specs = (P(("groups", "rows"), "cols", None), P(), P())
    out_specs = P(("groups", "rows"), "cols", None)
    return jax.shard_map(
        on_device, mesh=mesh, in_specs=in_specs, out_specs=out_specs, check_vma=False
    )
```

```python
import functools

import jax
import jax.numpy as jnp
from jax import lax
from jax.experimental import pallas as pl
from jax.experimental.pallas import tpu as pltpu
from jax.sharding import PartitionSpec as P

MESH = pl.DeviceIdType.MESH
NEAR, FAR = 2, 4
HALO = NEAR + FAR
PAD, PACK = 16, 8
SIDES = [(-1, 0), (1, 0), (0, -1), (0, 1), (-1, -1), (-1, 1), (1, -1), (1, 1)]


def extended(cells, sides, width):
    for axis, dim in sides:
        count = lax.axis_size(axis)
        ends = count - 1
        head = lax.slice_in_dim(cells, 0, width, axis=dim)
        tail = lax.slice_in_dim(cells, cells.shape[dim] - width, cells.shape[dim], axis=dim)
        cells = jnp.concatenate(
            [
                lax.ppermute(tail, axis, [(i, (i + 1) % count) for i in range(ends)]),
                cells,
                lax.ppermute(head, axis, [((i + 1) % count, i) for i in range(ends)]),
            ],
            axis=dim,
        )
    return cells


def valid_conv(padded, kernel, spread):
    out = lax.conv_general_dilated(
        padded[None],
        kernel,
        (1, 1),
        "VALID",
        rhs_dilation=(spread, spread),
        dimension_numbers=("NHWC", "HWIO", "NHWC"),
        preferred_element_type=jnp.float32,
    )
    return out[0]


def average(block_out, flipped):
    return ((block_out.astype(jnp.float32) + flipped.astype(jnp.float32)) * 0.5).astype(
        jnp.bfloat16
    )


def by_rows(contact_map, w_near, w_far):
    blocks = w_near.shape[0]
    state = lax.all_to_all(contact_map, "cols", split_axis=0, concat_axis=1, tiled=True)
    for block in range(blocks):
        padded = extended(state, ((("rows", "cols"), 0),), NEAR)
        padded = jnp.pad(padded, ((0, 0), (NEAR, NEAR), (0, 0)))
        hidden = jax.nn.relu(valid_conv(padded, w_near[block], NEAR)).astype(jnp.bfloat16)
        padded = extended(hidden, ((("rows", "cols"), 0),), FAR)
        padded = jnp.pad(padded, ((0, 0), (FAR, FAR), (0, 0)))
        block_out = (state.astype(jnp.float32) + valid_conv(padded, w_far[block], FAR)).astype(
            jnp.bfloat16
        )
        mirrored = lax.all_to_all(
            block_out, ("rows", "cols"), split_axis=1, concat_axis=0, tiled=True
        )
        state = average(block_out, jnp.swapaxes(mirrored, 0, 1))
    return lax.all_to_all(state, "cols", split_axis=1, concat_axis=0, tiled=True)


def flip(cells):
    return jnp.transpose(cells, (1, 0, 2))


def tile_kernel(
    count, side, x_ref, near_ref, far_ref, out_ref,
    pads, turned, strips, corners, mirror, hidden, near, far,
    load_sem, send_sem, recv_sem, mirror_sem,
):
    blocks, channels = near_ref.shape[0], near_ref.shape[-1]
    row, col = lax.axis_index("rows"), lax.axis_index("cols")
    last = count - 1
    inner = slice(HALO, HALO + side)
    body = slice(PAD, PAD + side)
    reach = side + 2 * FAR
    span = side + PAD
    half = side // 2

    load = pltpu.make_async_copy(x_ref, pads.at[0, inner, body], load_sem.at[0])
    load.start()

    def there(step):
        di, dj = step
        ok = []
        if di:
            ok.append(row > 0 if di < 0 else row < last)
        if dj:
            ok.append(col > 0 if dj < 0 else col < last)
        return ok[0] if len(ok) == 1 else jnp.logical_and(*ok)

    barrier = pltpu.get_barrier_semaphore()
    friends = (row != col).astype(jnp.int32)

    @pl.when(row != col)
    def _():
        pl.semaphore_signal(
            barrier, inc=1, device_id={"rows": col, "cols": row}, device_id_type=MESH
        )

    for step in SIDES:
        yes = there(step)
        friends += yes.astype(jnp.int32)

        @pl.when(yes)
        def _():
            pl.semaphore_signal(
                barrier, inc=1, device_id={"rows": row + step[0], "cols": col + step[1]},
                device_id_type=MESH,
            )

    def weight_loads(n):
        return (
            pltpu.make_async_copy(near_ref.at[n], near.at[n], load_sem.at[1 + 2 * n]),
            pltpu.make_async_copy(far_ref.at[n], far.at[n], load_sem.at[2 + 2 * n]),
        )

    def clear(ref):
        ref[...] = jnp.zeros(ref.shape, ref.dtype)

    def clear_off_map(ref, height, left, width):
        for at_edge, part in (
            (row == 0, (slice(0, height), slice(None))),
            (row == last, (slice(height + side, height * 2 + side), slice(None))),
            (col == 0, (slice(None), slice(left - width, left))),
            (col == last, (slice(None), slice(left + side, left + side + width))),
        ):
            pl.when(at_edge)(functools.partial(clear, ref.at[part]))

    def rim_copy(n, at):
        di, dj = SIDES[at]
        if di and dj:
            source, target = corners.at[n, 0, at], corners.at[n, 1, at]
        elif di:
            rows = slice(HALO, 2 * HALO) if di < 0 else slice(side, side + HALO)
            to = slice(HALO + side, 2 * HALO + side) if di < 0 else slice(0, HALO)
            source, target = pads.at[n, rows, body], pads.at[n, to, body]
        else:
            source = turned.at[n, slice(0, HALO) if dj < 0 else slice(side - HALO, side)]
            target = strips.at[n, 1 if dj < 0 else 0]
        return pltpu.make_async_remote_copy(
            src_ref=source, dst_ref=target,
            send_sem=send_sem.at[n, at], recv_sem=recv_sem.at[n, at],
            device_id={"rows": row + di, "cols": col + dj}, device_id_type=MESH,
        )

    def rim_start(n, ats):
        for at in ats:
            @pl.when(there(SIDES[at]))
            def _():
                rim_copy(n, at).start()

    def pack_corners(n, end):
        bins = slice(0, HALO) if end == 0 else slice(side - HALO, side)
        for at in (4 + end, 6 + end):
            rows = slice(0, PACK) if SIDES[at][0] < 0 else slice(side - PACK, side)
            corners[n, 0, at] = turned[n, bins, rows].reshape(HALO * PACK, channels)

    def rim_sent(n):
        for at, step in enumerate(SIDES):
            @pl.when(there(step))
            def _():
                rim_copy(n, at).wait_send()

    def wait_columns(n):
        for at in (2, 3):
            dj = SIDES[at][1]

            @pl.when(there((0, -dj)))
            def _():
                rim_copy(n, at).wait_recv()
                bins = slice(PAD - HALO, PAD) if dj > 0 else slice(
                    PAD + side, PAD + side + HALO)
                pads[n, inner, bins] = flip(strips[n, 0 if dj > 0 else 1])

    def wait_rows(n, above):
        down = above.astype(jnp.int32)
        rows = pl.ds(jnp.where(above, 0, HALO + side), HALO)

        def landed(ref, at):
            pltpu.make_async_remote_copy(
                src_ref=ref, dst_ref=ref,
                send_sem=send_sem.at[n, at], recv_sem=recv_sem.at[n, at],
                device_id={"rows": row, "cols": col}, device_id_type=MESH,
            ).wait_recv()

        @pl.when(jnp.where(above, row, last - row) > 0)
        def _():
            landed(pads.at[n, rows, body], down)
            for right, dj in enumerate((-1, 1)):
                at = 4 + 2 * down + right

                @pl.when(col < last if dj < 0 else col > 0)
                def _():
                    landed(corners.at[n, 1, at], at)
                    bins = slice(PAD - HALO, PAD) if dj > 0 else slice(
                        PAD + side, PAD + side + HALO)
                    corner = flip(corners[n, 1, at].reshape(HALO, PACK, channels))
                    pads[n, rows, bins] = jnp.where(
                        above, corner[PACK - HALO:], corner[:HALO])

    def hidden_rows(n, weights, start, size):
        first, wide = PAD - HALO, weights.shape[1]
        shifted = [
            pads[n, pl.ds(start, size + 2 * NEAR), first + NEAR * b:first + NEAR * b + span]
            for b in range(3)
        ]
        taps = [
            shifted[b][NEAR * a:NEAR * a + size].reshape(size * span, channels)
            for a in range(3) for b in range(3)
        ]
        total = jnp.dot(
            jnp.concatenate(taps, axis=1), weights, preferred_element_type=jnp.float32
        )
        hidden[pl.ds(start, size), :, :wide] = (
            jnp.maximum(total, 0.0).astype(hidden.dtype).reshape(size, span, wide)
        )

    def far_sum(lanes, weights, start):
        taps = []
        for lane in lanes:
            part = slice(lane * channels, (lane + 1) * channels)
            shifted = [
                hidden[pl.ds(start, half + 2 * FAR), FAR * b:FAR * b + side, part]
                for b in range(3)
            ]
            taps += [
                shifted[b][FAR * a:FAR * a + half].reshape(half * side, channels)
                for a in range(3) for b in range(3)
            ]
        return jnp.dot(
            jnp.concatenate(taps, axis=1), weights, preferred_element_type=jnp.float32
        ).reshape(half, side, channels)

    def own_rows(n, start):
        return pads[n, pl.ds(HALO + start, half), body].astype(jnp.float32)

    def halves_of(n, weights, half_done):
        wait_columns(n)
        for copy in weight_loads(n):
            copy.wait()
        middle = -(-(side - 2 * NEAR) // HALO)

        @pl.loop(0, middle + 2)
        def _(step):
            k = step - middle
            above = lax.rem(row, 2) == 1 - k

            @pl.when(k >= 0)
            def _():
                wait_rows(n, above)

            between = jnp.minimum(HALO * (step + 1), reach - 2 * HALO)
            ends = jnp.where(above, 0, reach - HALO)
            hidden_rows(n, weights(), jnp.where(k < 0, between, ends), HALO)

            @pl.when(k >= 0)
            def _():
                clear_off_map(hidden, FAR, FAR, FAR)
                half_done(k, jnp.where(above, 0, half))

    def straight(w, n):
        return w[n].reshape(9 * channels, channels)

    def crossed(w, n):
        return jnp.concatenate([w[n, b, a] for a in range(3) for b in range(3)], axis=0)

    for n in range(blocks):
        clear_off_map(pads.at[n], HALO, PAD, PAD)

    def swap(k, start):
        part = pl.ds(start, half)
        return pltpu.make_async_remote_copy(
            src_ref=mirror.at[0, part], dst_ref=mirror.at[1, part],
            send_sem=mirror_sem.at[0, k], recv_sem=mirror_sem.at[1, k],
            device_id={"rows": col, "cols": row}, device_id_type=MESH,
        )

    def mirror_half(k, start):
        part = pl.ds(start, half)
        total = far_sum((0,), straight(far, 0), start)
        mirror[0, part] = (own_rows(0, start) + total).astype(mirror.dtype)

        @pl.when(row != col)
        def _():
            swap(k, start).start()

        @pl.when(row == col)
        def _():
            mirror[1, part] = mirror[0, part]

    def end_of(k):
        return jnp.where(lax.rem(col, 2) == 1 - k, 0, 1)

    def columns_half(n, k):
        part = pl.ds(end_of(k) * half, half)

        @pl.when(row != col)
        def _():
            swap(k, end_of(k) * half).wait_recv()

        turned[n, part] = average(turned[n, part], mirror[1, part])

    def send_end(n, end):
        for which in range(2):
            @pl.when(end == which)
            def _():
                rim_start(n, (2 + which,))
                pack_corners(n, which)
                rim_start(n, (4 + which, 6 + which))

    def average_half(n, k, start):
        weights = jnp.concatenate([straight(far, n), crossed(far, n)], axis=0)
        total = far_sum((0, 1), weights, start)
        value = (own_rows(n, start) + total * 0.5).astype(out_ref.dtype)
        if n == blocks - 1:
            out_ref[pl.ds(start, half)] = value
        else:
            pads[n + 1, pl.ds(HALO + start, half), body] = value

    def mirror_sent():
        @pl.when(row != col)
        def _():
            for k in range(2):
                swap(k, jnp.where(lax.rem(row, 2) == 1 - k, 0, half)).wait_send()

    load.wait()
    for copy in weight_loads(0):
        copy.start()
    state = pads[0, inner, body]
    turned[0] = flip(state)
    pack_corners(0, 0)
    pack_corners(0, 1)
    pl.semaphore_wait(barrier, friends)
    rim_start(0, (2, 3, 0, 1, 4, 5, 6, 7))

    for n in range(blocks):
        if n == 0:
            halves_of(n, lambda: straight(near, n), mirror_half)
            for copy in weight_loads(n + 1):
                copy.start()
            turned[n + 1] = flip(mirror[0])
            rim_sent(n)
            columns_half(n + 1, 0)
            send_end(n + 1, end_of(0))
            columns_half(n + 1, 1)
            state = flip(turned[n + 1])
            pads[n + 1, inner, body] = state
            rim_start(n + 1, (0, 1))
            send_end(n + 1, end_of(1))
            mirror_sent()
        else:
            halves_of(
                n, lambda: jnp.concatenate([straight(near, n), crossed(near, n)], axis=1),
                functools.partial(average_half, n),
            )
            rim_sent(n)
            if n < blocks - 1:
                for copy in weight_loads(n + 1):
                    copy.start()
                state = pads[n + 1, inner, body]
                turned[n + 1] = flip(state)
                pack_corners(n + 1, 0)
                pack_corners(n + 1, 1)
                rim_start(n + 1, (2, 3, 0, 1, 4, 5, 6, 7))


def by_tiles(contact_map, w_near, w_far):
    blocks, channels = w_near.shape[0], w_near.shape[-1]
    side, count = contact_map.shape[0], lax.axis_size("rows")
    kind = contact_map.dtype
    return pl.pallas_call(
        functools.partial(tile_kernel, count, side),
        out_shape=jax.ShapeDtypeStruct(contact_map.shape, kind),
        in_specs=[pl.BlockSpec(memory_space=pltpu.HBM)] * 3,
        out_specs=pl.BlockSpec(memory_space=pltpu.VMEM),
        scratch_shapes=[
            pltpu.VMEM((blocks, side + 2 * HALO, side + 2 * PAD, channels), kind),
            pltpu.VMEM((blocks, side, side, channels), kind),
            pltpu.VMEM((blocks, 2, HALO, side, channels), kind),
            pltpu.VMEM((blocks, 2, len(SIDES), HALO * PACK, channels), kind),
            pltpu.VMEM((2, side, side, channels), kind),
            pltpu.VMEM((side + 2 * FAR, side + PAD, 2 * channels), kind),
            pltpu.VMEM(w_near.shape, kind),
            pltpu.VMEM(w_far.shape, kind),
            pltpu.SemaphoreType.DMA((1 + 2 * blocks,)),
            pltpu.SemaphoreType.DMA((blocks, len(SIDES))),
            pltpu.SemaphoreType.DMA((blocks, len(SIDES))),
            pltpu.SemaphoreType.DMA((2, 2)),
        ],
        compiler_params=pltpu.CompilerParams(
            collective_id=0, has_side_effects=True, vmem_limit_bytes=431 * 2**17
        ),
    )(contact_map, w_near, w_far)


def on_device(contact_map, w_near, w_far):
    side = contact_map.shape[0]
    square = side == contact_map.shape[1] and side % PAD == 0
    if square and lax.axis_size("rows") == lax.axis_size("cols") and w_near.shape[0] > 1:
        return by_tiles(contact_map, w_near, w_far)
    return by_rows(contact_map, w_near, w_far)


def solution(mesh):
    in_specs = (P(("groups", "rows"), "cols", None), P(), P())
    out_specs = P(("groups", "rows"), "cols", None)
    return jax.shard_map(
        on_device, mesh=mesh, in_specs=in_specs, out_specs=out_specs, check_vma=False
    )
```
